32 devices in a mesh: ctx: 2 (over core), ex: 16 (over z, y, x).
Axes of the slice: x: 2, y: 2, z: 4, core: 2. Of those that a mesh axis runs over, the one named last changes fastest.
Arguments:
- acts: bfloat16 [16, 256, 8192], P('ex', 'ctx'), may hold values from -6 to 6
- out_grads: bfloat16 [16, 256, 8192], P('ex', 'ctx'), may hold values from -6 to 6
- projections: bfloat16 [2, 8192, 256], P(None, 'ex', 'ctx'), may hold values from -0.0625 to 0.0625
- segments: int32 [16, 256], P('ex', 'ctx'), may hold values from 0 to 3, never falling along the last dimension, each value on 1 to 128 neighbouring positions
- valid: int32 [16, 256], P('ex', 'ctx'), may hold values 0 or 1
- stored: bfloat16 [49152, 8192], P('ex', 'ctx'), may hold values from -60 to 60, as said below
Outputs:
- scores: float32 [64, 49152], P('ctx', 'ex')
The draws below stay inside these ranges and needn't reach their ends.
Inputs may be any that keep to these rules, and one draw needn't show every extreme that they name: `stored`: finite real values.
All inputs are finite; a program needn't handle non-finite values. No bound on the sum of `valid` on one device may be relied on, other than what follows from the above.
Results may differ from the reference program's by a relative error of at most 0.005.
Values may be sent and summed in bfloat16 or wider, within the bound.
No kernel may reach another device: no remote copies, remote signals or barrier semaphores. Data moves between devices by JAX's collectives and lax.ppermute only.
A program may use at most 128 MiB of HBM per device.

```python
import math
import jax
import jax.numpy as jnp
import numpy as np
from jax import lax

D = 8192
RANK = 32
MODULES = 8
FEAT = 1024
DOCS = 4
STEPS = 4
LEN = 256
STORE = 49152
N_EX = 16


def draw_stored(key, part):
    key = jax.random.fold_in(key, 11)
    key_entries, key_rough = jax.random.split(key)
    positions = jnp.arange(STORE).astype(jnp.float32)
    rising = jnp.exp(math.log(3.0) * positions / (STORE - 1))
    entries = jax.random.truncated_normal(key_entries, -4.0, 4.0, (STORE, MODULES * FEAT), jnp.float32)
    rough = jnp.exp(jax.random.uniform(key_rough, (STORE,), jnp.float32, -0.35, 0.35))
    return (entries * (rising * rough)[:, None]).astype(jnp.bfloat16)


def set_ends(array, own_key, low, largest):
    index_at = [jax.random.randint(jax.random.fold_in(own_key, axis), (), 0, length) for axis, length in enumerate(array.shape)]
    widest = array.shape.index(max(array.shape))
    beside = index_at[:widest] + [(index_at[widest] + 1) % array.shape[widest]] + index_at[widest + 1:]
    return array.at[tuple(index_at)].set(low).at[tuple(beside)].set(largest)


def level_of(own_key, dims, cuts, least, top_value):
    def one(dim, blocks):
        steps = jax.random.uniform(jax.random.fold_in(jax.random.fold_in(own_key, 6), dim), (blocks,), jnp.float32, least / len(cuts), top_value / len(cuts))
        return jnp.repeat(jnp.exp(steps), dims[dim] // blocks).reshape((-1,) + (1,) * (len(dims) - dim - 1))

    gain = one(*cuts[0])
    for cut in cuts[1:]:
        gain = gain * one(*cut)
    return gain


def split_up(number_of, total, bound, slope):
    loads = [(1 << 20) // math.isqrt(rank ** slope) + 1 for rank in range(2, number_of + 1)]
    surplus, given = total - bound - (number_of - 1), [1] * (number_of - 1)
    while surplus > 0:
        free = [i for i in range(number_of - 1) if given[i] < bound]
        whole, left = sum([loads[i] for i in free]), surplus
        for i in free:
            addition = min(bound - given[i], max(1, left * loads[i] // whole), surplus)
            given[i] = given[i] + addition
            surplus = surplus - addition
    return np.array([bound] + given)


def ragged_sizes(rng, amount, total, most, skew):
    if amount == 2:
        one = jax.random.randint(rng, (), max(1, total - most), min(most, total - 1) + 1)
        return jnp.stack([one, total - one])
    sizes = jnp.asarray(split_up(amount, total, most, skew), jnp.int32)
    pairs = (amount - 1) // 2
    source_of, sink = sizes[1:1 + 2 * pairs:2], sizes[2:2 + 2 * pairs:2]
    margin = jnp.minimum(source_of - 1, most - sink)
    shifted = jax.random.randint(jax.random.fold_in(rng, 1), (pairs,), 0, 1 << 20) % (margin + 1)
    sizes = sizes.at[1:1 + 2 * pairs:2].set(source_of - shifted).at[2:2 + 2 * pairs:2].set(sink + shifted)
    return sizes[jax.random.permutation(jax.random.fold_in(rng, 2), amount)]


def noise(rng, shape, scale, bound, shards=(), kind=jnp.bfloat16):
    drawn = jax.random.normal(rng, shape, jnp.float32) * scale
    if len(shards) > 0:
        drawn = level_of(rng, shape, shards, -0.22, 0.18) * drawn
    return jnp.clip(drawn, min=-bound, max=bound).astype(kind)


def setup_inputs(seed: int = 0) -> dict:
    seeds = jax.random.split(jax.random.key(seed), 7)
    return {
        "acts": noise(seeds[0], (N_EX, LEN, D), 1.0, 6.0, ((0, 16), (1, 2))),
        "out_grads": noise(seeds[1], (N_EX, LEN, D), 1.0, 6.0, ((0, 16), (1, 2))),
        "projections": noise(seeds[2], (2, D, MODULES * RANK), D ** -0.5, 0.0625, ((1, 16), (2, 2))),
        "segments": jax.vmap(lambda own: jnp.searchsorted(jnp.cumsum(ragged_sizes(own, DOCS, LEN, LEN // 2, 1)), jnp.arange(LEN), side="right"))(jax.random.split(seeds[3], N_EX)).reshape((N_EX, LEN)).astype(jnp.int32),
        "valid": set_ends((jax.random.randint(seeds[4], (N_EX, LEN), 0, 8) < 7).astype(jnp.int32), jax.random.fold_in(seeds[4], 1), 0, 1),
        "stored": draw_stored(jax.random.fold_in(seeds[6], 71), 0),
    }


damping = 0.1
spread = 1.5
epsilon = 1e-06

def reference(acts, out_grads, projections, segments, valid, stored):
    doc_ids = jnp.arange(DOCS, dtype=jnp.int32)

    def one_context(packed):
        x_rows, g_rows, seg_rows, ok_rows = packed
        x_proj = jnp.dot(x_rows, projections[0], preferred_element_type=jnp.float32).astype(jnp.bfloat16)
        g_proj = jnp.dot(g_rows, projections[1], preferred_element_type=jnp.float32).astype(jnp.bfloat16)
        onehot = ((seg_rows[None, :] == doc_ids[:, None]) & (ok_rows[None, :] == 1)).astype(jnp.bfloat16)
        weighted = (onehot[:, :, None] * g_proj[None, :, :]).reshape(DOCS, LEN, MODULES, RANK)
        summed = jnp.einsum('qtmi,tmj->qmij', weighted.astype(jnp.float32), x_proj.reshape(LEN, MODULES, RANK).astype(jnp.float32))
        return summed.reshape(DOCS, MODULES, FEAT)
    queries = lax.map(one_context, (acts, out_grads, segments, valid)).reshape(N_EX * DOCS, MODULES, FEAT)

    def module_gram(module):
        columns = lax.dynamic_slice_in_dim(stored, module * FEAT, FEAT, 1)
        return jnp.dot(columns.T, columns, preferred_element_type=jnp.float32) / STORE
    curvature = lax.map(module_gram, jnp.arange(MODULES, dtype=jnp.int32))
    mean_diag = jnp.trace(curvature, axis1=1, axis2=2) / FEAT
    step_size = (1.0 / (spread * (mean_diag + epsilon)))[None, :, None]

    def apply_fisher(iterate):
        return jnp.einsum('mfg,qmg->qmf', curvature, iterate, precision=lax.Precision.HIGHEST) + damping * mean_diag[None, :, None] * iterate
    iterate = step_size * queries
    for iteration in range(STEPS):
        iterate = iterate + step_size * (queries - apply_fisher(iterate))
    precond = iterate.astype(jnp.bfloat16).reshape(N_EX * DOCS, MODULES * FEAT)
    score_scale = 1.0 / math.sqrt(MODULES * FEAT * LEN / DOCS)
    raw_scores = lax.dot_general(precond, stored, (((1,), (1,)), ((), ())), preferred_element_type=jnp.float32)
    return raw_scores * score_scale
```

```python
import functools
import math

import jax
import jax.numpy as jnp
from jax import lax
from jax.experimental import pallas as pl
from jax.experimental.pallas import tpu as pltpu
from jax.sharding import PartitionSpec as P

RANK = 32
MODULES = 8
DOCS = 4
STEPS = 4
FEAT = RANK * RANK
HALF = FEAT // 2
BLOCK = FEAT // 4
EXTRA = 16

damping = 0.1
spread = 1.5
epsilon = 1e-06


def gram_kernel(s_ref, out_ref, diag_ref, ab_ref, c_ref):
    k = pl.program_id(1)

    @pl.when(k == 0)
    def _():
        ab_ref[...] = jnp.zeros_like(ab_ref)
        c_ref[...] = jnp.zeros_like(c_ref)

    rows = s_ref[...]
    contract = (((0,), (0,)), ((), ()))
    ab_ref[...] += lax.dot_general(
        rows[:, :HALF], rows, contract, preferred_element_type=jnp.float32
    )
    c_ref[...] += lax.dot_general(
        rows[:, HALF:], rows[:, HALF:], contract, preferred_element_type=jnp.float32
    )

    @pl.when(k == pl.num_programs(1) - 1)
    def _():
        at_row = lax.broadcasted_iota(jnp.int32, (HALF, HALF), 0)
        at_col = lax.broadcasted_iota(jnp.int32, (HALF, HALF), 1)
        a = ab_ref[:, :HALF]
        c = c_ref[...]
        out_ref[0, :HALF] = ab_ref[:, HALF:].astype(jnp.bfloat16)
        out_ref[0, HALF:] = jnp.where(at_row < at_col, a, c).astype(jnp.bfloat16)
        on = at_row == at_col
        diag_ref[0, :, :HALF] = jnp.sum(jnp.where(on, a, 0.0), axis=0, keepdims=True)
        diag_ref[0, :, HALF:] = jnp.sum(jnp.where(on, c, 0.0), axis=0, keepdims=True)


def packed_gram(stored):
    rows, cols = stored.shape
    modules = cols // FEAT
    depth = 1024
    while rows % depth:
        depth //= 2
    return pl.pallas_call(
        gram_kernel,
        grid=(modules, rows // depth),
        in_specs=[pl.BlockSpec((depth, FEAT), lambda m, k: (k, m))],
        out_specs=[
            pl.BlockSpec((1, FEAT, HALF), lambda m, k: (m, 0, 0)),
            pl.BlockSpec((1, 1, FEAT), lambda m, k: (m, 0, 0)),
        ],
        out_shape=[
            jax.ShapeDtypeStruct((modules, FEAT, HALF), jnp.bfloat16),
            jax.ShapeDtypeStruct((modules, 1, FEAT), jnp.float32),
        ],
        scratch_shapes=[
            pltpu.VMEM((HALF, FEAT), jnp.float32),
            pltpu.VMEM((HALF, HALF), jnp.float32),
        ],
        compiler_params=pltpu.CompilerParams(vmem_limit_bytes=32 * 1024 * 1024),
        cost_estimate=pl.CostEstimate(
            flops=2 * rows * FEAT * FEAT * modules * 3 // 4,
            bytes_accessed=rows * cols * 2 + modules * FEAT * HALF * 2,
            transcendentals=0,
        ),
        name="gram",
    )(stored)


def richardson_kernel(total_rows, packed_ref, diag_ref, q_ref, out_ref, full_ref):
    at_row = lax.broadcasted_iota(jnp.int32, (HALF, HALF), 0)
    at_col = lax.broadcasted_iota(jnp.int32, (HALF, HALF), 1)
    both = packed_ref[HALF:].astype(jnp.float32)
    both_t = both.T
    zero = jnp.zeros_like(both)
    above, below = at_row < at_col, at_row > at_col
    full_ref[:HALF, :HALF] = jnp.where(above, both, jnp.where(below, both_t, zero)).astype(jnp.bfloat16)
    full_ref[HALF:, HALF:] = jnp.where(below, both, jnp.where(above, both_t, zero)).astype(jnp.bfloat16)
    cross = packed_ref[:HALF]
    full_ref[:HALF, HALF:] = cross
    full_ref[HALF:, :HALF] = cross.astype(jnp.float32).T.astype(jnp.bfloat16)
    diag = diag_ref[...] / total_rows
    mean_diag = jnp.sum(diag, axis=1, keepdims=True) / FEAT
    step_size = 1.0 / (spread * (mean_diag + epsilon))
    own = diag + damping * mean_diag
    queries = q_ref[...]
    count = queries.shape[0]
    v = step_size * queries
    for _ in range(STEPS):
        high = v.astype(jnp.bfloat16)
        rest = v - high.astype(jnp.float32)
        mid = rest.astype(jnp.bfloat16)
        low = (rest - mid.astype(jnp.float32)).astype(jnp.bfloat16)
        parts = jnp.concatenate([high, mid, low], axis=0)
        off = jnp.dot(parts, full_ref[...], preferred_element_type=jnp.float32)
        off = off[:count] + (off[count : 2 * count] + off[2 * count :])
        v = v + step_size * (queries - (off / total_rows + own * v))
    out_ref[...] = v.astype(jnp.bfloat16)


def precondition(total_rows, packed, diag, queries):
    count = queries.shape[0]
    return pl.pallas_call(
        functools.partial(richardson_kernel, total_rows),
        out_shape=jax.ShapeDtypeStruct((count, FEAT), jnp.bfloat16),
        scratch_shapes=[pltpu.VMEM((FEAT, FEAT), jnp.bfloat16)],
        compiler_params=pltpu.CompilerParams(vmem_limit_bytes=32 * 1024 * 1024),
        cost_estimate=pl.CostEstimate(
            flops=2 * STEPS * 3 * count * FEAT * FEAT, bytes_accessed=4 * FEAT * FEAT, transcendentals=0
        ),
        name="richardson",
    )(packed, diag, queries)


def swapped(value, n_ctx):
    return [value] + [
        lax.ppermute(value, "ctx", [(i, (i + s) % n_ctx) for i in range(n_ctx)])
        for s in range(1, n_ctx)
    ]


def general(acts, out_grads, projections, segments, valid, stored):
    n_ex = lax.axis_size("ex")
    n_ctx = lax.axis_size("ctx")
    tok_count = acts.shape[1]
    mod_dev = projections.shape[2] // RANK
    owners = n_ex // mod_dev
    me = lax.axis_index("ex")

    weights = [lax.all_gather(projections[i], "ex", axis=0, tiled=True) for i in range(2)]
    x_parts = swapped(acts[0], n_ctx)
    g_parts = swapped(out_grads[0], n_ctx)
    marks = swapped(jnp.concatenate([segments, valid], axis=0), n_ctx)

    packed, diag = packed_gram(stored)
    sums = lax.psum_scatter(
        packed.reshape(n_ex, FEAT // owners, HALF), "ex", scatter_dimension=0, tiled=True
    )[0]
    diag = lax.psum(diag, "ex")
    groups = [list(range(m * owners, (m + 1) * owners)) for m in range(mod_dev)]
    packed_mine = lax.all_gather(sums, "ex", axis=0, tiled=True, axis_index_groups=groups)
    my_module = me // owners
    diag_mine = lax.dynamic_index_in_dim(diag, my_module, 0, keepdims=False)

    queries = 0.0
    doc_ids = jnp.arange(DOCS, dtype=jnp.int32)
    for x_rows, g_rows, mark in zip(x_parts, g_parts, marks):
        xp = jnp.dot(x_rows, weights[0], preferred_element_type=jnp.float32).astype(jnp.bfloat16)
        gp = jnp.dot(g_rows, weights[1], preferred_element_type=jnp.float32).astype(jnp.bfloat16)
        onehot = ((mark[0][None, :] == doc_ids[:, None]) & (mark[1][None, :] == 1)).astype(jnp.bfloat16)
        weighted = (onehot[:, :, None] * gp[None, :, :]).reshape(DOCS, tok_count, mod_dev, RANK)
        queries = queries + jnp.einsum(
            "qtmi,tmj->mqij",
            weighted,
            xp.reshape(tok_count, mod_dev, RANK),
            preferred_element_type=jnp.float32,
        )
    queries = queries.reshape(mod_dev, DOCS, FEAT)

    place = lax.rem(me, mod_dev)
    arrived = []
    for j in range(mod_dev):
        module = lax.rem(place + j, mod_dev)
        part = lax.dynamic_index_in_dim(queries, module, 0, keepdims=False)
        pairs = [
            (e, ((e % mod_dev + j) % mod_dev) * owners + e // mod_dev) for e in range(n_ex)
        ]
        arrived.append(lax.ppermute(part, "ex", pairs))
    arrived = jnp.stack(arrived)
    order = lax.rem(my_module - jnp.arange(mod_dev) + mod_dev, mod_dev)
    mine = jnp.take(arrived, order, axis=0).reshape(mod_dev * DOCS, FEAT)

    total_rows = stored.shape[0] * n_ex
    precond = precondition(float(total_rows), packed_mine, diag_mine, mine)

    flat = lax.all_gather(precond, "ex", axis=0, tiled=True).reshape(mod_dev, n_ex * DOCS, FEAT)
    flat = jnp.transpose(flat, (1, 0, 2)).reshape(n_ex * DOCS, mod_dev * FEAT)
    score_scale = 1.0 / math.sqrt(MODULES * FEAT * tok_count * n_ctx / DOCS)
    summed = lax.psum_scatter(
        lax.dot_general(flat, stored, (((1,), (1,)), ((), ())), preferred_element_type=jnp.float32),
        "ctx",
        scatter_dimension=0,
        tiled=True,
    )
    return summed * score_scale


def vmem_params():
    return pltpu.CompilerParams(vmem_limit_bytes=32 * 1024 * 1024)


def small_cost(*arrays):
    return pl.CostEstimate(
        flops=0, bytes_accessed=sum(math.prod(a.shape) * a.dtype.itemsize for a in arrays), transcendentals=0
    )


def rows_of_diag(diag):
    high = diag.astype(jnp.bfloat16)
    rest = diag - high.astype(jnp.float32)
    mid = rest.astype(jnp.bfloat16)
    low = (rest - mid.astype(jnp.float32)).astype(jnp.bfloat16)
    empty = jnp.zeros((EXTRA - 3 * diag.shape[0], HALF), jnp.float32)
    terms = [t.astype(jnp.float32) for t in (high, mid, low)]
    return jnp.concatenate(terms + [empty], axis=0).astype(jnp.bfloat16)


def diag_of_rows(rows):
    terms = rows.astype(jnp.float32)
    return terms[0:2] + (terms[2:4] + terms[4:6])


def block_gram_kernel(ties, meta_ref, s_ref, *refs):
    o0, o1, o2, o3a, o3b, extra_ref, ab_ref, c_ref, pay_ref = refs[ties:]
    k = pl.program_id(0)

    @pl.when(k == 0)
    def _():
        ab_ref[...] = jnp.zeros_like(ab_ref)
        c_ref[...] = jnp.zeros_like(c_ref)

    rows = s_ref[...]
    contract = (((0,), (0,)), ((), ()))
    ab_ref[...] += lax.dot_general(
        rows[:, :HALF], rows, contract, preferred_element_type=jnp.float32
    )
    c_ref[...] += lax.dot_general(
        rows[:, HALF:], rows[:, HALF:], contract, preferred_element_type=jnp.float32
    )

    @pl.when(k == pl.num_programs(0) - 1)
    def _():
        at_row = lax.broadcasted_iota(jnp.int32, (HALF, HALF), 0)
        at_col = lax.broadcasted_iota(jnp.int32, (HALF, HALF), 1)
        a = ab_ref[:, :HALF]
        c = c_ref[...]
        cross = ab_ref[:, HALF:].astype(jnp.bfloat16)
        both = jnp.where(at_row < at_col, a, c).astype(jnp.bfloat16)
        pay_ref[0] = cross[:BLOCK]
        pay_ref[1] = cross[BLOCK:]
        pay_ref[2] = both[:BLOCK]
        pay_ref[3] = both[BLOCK:]
        on = at_row == at_col
        diag_a = jnp.sum(jnp.where(on, a, 0.0), axis=0, keepdims=True)
        diag_c = jnp.sum(jnp.where(on, c, 0.0), axis=0, keepdims=True)
        extra_ref[...] = rows_of_diag(jnp.concatenate([diag_a, diag_c], axis=0))
        o0[...] = pay_ref[meta_ref[1]]
        o1[...] = pay_ref[meta_ref[2]]
        o2[...] = pay_ref[meta_ref[3]]
        o3a[...] = pay_ref[meta_ref[4], : BLOCK // 2]
        o3b[...] = pay_ref[meta_ref[4], BLOCK // 2 :]


def block_gram(stored, module, corner, ties):
    rows = stored.shape[0]
    depth = 1024
    while rows % depth:
        depth //= 2
    meta = jnp.stack([module] + [corner ^ j for j in range(4)]).astype(jnp.int32)
    heights = [BLOCK, BLOCK, BLOCK, BLOCK // 2, BLOCK // 2, EXTRA]
    return pl.pallas_call(
        functools.partial(block_gram_kernel, len(ties)),
        grid_spec=pltpu.PrefetchScalarGridSpec(
            num_scalar_prefetch=1,
            grid=(rows // depth,),
            in_specs=[pl.BlockSpec((depth, FEAT), lambda k, meta: (k, meta[0]))]
            + [pl.BlockSpec(memory_space=pl.ANY)] * len(ties),
            out_specs=[pl.BlockSpec((h, HALF), lambda k, meta: (0, 0)) for h in heights],
            scratch_shapes=[
                pltpu.VMEM((HALF, FEAT), jnp.float32),
                pltpu.VMEM((HALF, HALF), jnp.float32),
                pltpu.VMEM((4, BLOCK, HALF), jnp.bfloat16),
            ],
        ),
        out_shape=[jax.ShapeDtypeStruct((h, HALF), jnp.bfloat16) for h in heights],
        compiler_params=vmem_params(),
        cost_estimate=pl.CostEstimate(
            flops=2 * rows * FEAT * FEAT * 3 // 4,
            bytes_accessed=rows * FEAT * 2 + FEAT * HALF * 2,
            transcendentals=0,
        ),
        name="gram",
    )(meta, stored, *ties)


def pass_kernel(o1, o2, from_x, from_y, for_x, for_y):
    half = BLOCK // 2
    f32 = jnp.float32
    for_x[:half] = o1[:half]
    for_x[half:] = (o1[half:].astype(f32) + from_y[...].astype(f32)).astype(jnp.bfloat16)
    for_y[:half] = (o2[:half].astype(f32) + from_x[...].astype(f32)).astype(jnp.bfloat16)
    for_y[half:] = o2[half:]


def pass_on(o1, o2, from_x, from_y):
    return pl.pallas_call(
        pass_kernel,
        out_shape=[jax.ShapeDtypeStruct(o1.shape, o1.dtype)] * 2,
        compiler_params=vmem_params(),
        cost_estimate=small_cost(o1, o2, o1, o2),
        name="pass_on",
    )(o1, o2, from_x, from_y)


def close_kernel(count, *refs):
    blocks, extra, arrived, out = refs[:3], refs[3], refs[4:-1], refs[-1]
    f32 = jnp.float32
    total = blocks[0][...].astype(f32) + blocks[1][...].astype(f32) + blocks[2][...].astype(f32)
    if not count:
        out[:BLOCK] = total.astype(jnp.bfloat16)
        out[BLOCK:] = extra[...]
        return
    diag = diag_of_rows(extra[...])
    for other in arrived:
        total = total + other[:BLOCK].astype(f32)
        diag = diag + diag_of_rows(other[BLOCK:])
    out[:BLOCK] = total.astype(jnp.bfloat16)
    out[BLOCK:] = rows_of_diag(diag)


def close(o0, got_x, got_y, extra, arrived=()):
    return pl.pallas_call(
        functools.partial(close_kernel, len(arrived)),
        out_shape=jax.ShapeDtypeStruct((BLOCK + EXTRA, HALF), jnp.bfloat16),
        compiler_params=vmem_params(),
        cost_estimate=small_cost(o0, got_x, got_y, *arrived),
        name="close",
    )(o0, got_x, got_y, extra, *arrived)


def project_kernel(has_total, meta_ref, *refs):
    own, across, along, opp0, opp1 = refs[:5]
    rest = refs[5:]
    total_in = None
    if has_total:
        total_in, rest = rest[0], rest[1:]
    out = rest[-1]
    rest = rest[:-1]
    parts = len(rest) // 8
    for which in range(2):
        for part in range(parts):
            total = None
            for corner in range(4):
                block = rest[(part * 2 + which) * 4 + corner][...]
                if corner < 3:
                    piece = (own, across, along)[corner][which]
                else:
                    piece = (opp0, opp1)[which][...]
                term = jnp.dot(block, piece, preferred_element_type=jnp.float32)
                total = term if total is None else total + term
            if has_total:
                total = total + total_in[which, part]
            out[which, part] = total


def project(pieces, x_parts, g_parts, line, corner, total):
    opp0 = pieces[3]
    depth, width = opp0.shape
    tok_count = x_parts[0].shape[0]
    meta = jnp.stack([4 * line + (corner ^ j) for j in range(4)]).astype(jnp.int32)

    def whole(shape):
        return pl.BlockSpec(shape, lambda i, meta: (0,) * len(shape))

    def columns(j):
        return pl.BlockSpec((tok_count, depth), lambda i, meta: (0, meta[j]))

    in_specs = [whole(p.shape) for p in pieces]
    operands = list(pieces)
    if total is not None:
        in_specs.append(whole(total.shape))
        operands.append(total)
    for x_rows, g_rows in zip(x_parts, g_parts):
        for rows in (x_rows, g_rows):
            for j in range(4):
                in_specs.append(columns(j))
                operands.append(rows)
    shape = (2, len(x_parts), tok_count, width)
    return pl.pallas_call(
        functools.partial(project_kernel, total is not None),
        grid_spec=pltpu.PrefetchScalarGridSpec(
            num_scalar_prefetch=1,
            grid=(1,),
            in_specs=in_specs,
            out_specs=whole(shape),
        ),
        out_shape=jax.ShapeDtypeStruct(shape, jnp.float32),
        compiler_params=vmem_params(),
        cost_estimate=pl.CostEstimate(
            flops=2 * 2 * len(x_parts) * tok_count * 4 * depth * width,
            bytes_accessed=2 * (2 * len(x_parts) * tok_count + 2 * width) * 4 * depth,
            transcendentals=0,
        ),
        name="project",
    )(meta, *operands)


def gradient_kernel(meta_ref, total_ref, *refs):
    parts = total_ref.shape[1]
    marks, outs = refs[:parts], refs[parts:]
    width = total_ref.shape[3]
    xp = jnp.concatenate([total_ref[0, p].astype(jnp.bfloat16) for p in range(parts)], axis=0)
    gp = jnp.concatenate([total_ref[1, p].astype(jnp.bfloat16) for p in range(parts)], axis=0)
    tok_count = total_ref.shape[2]
    doc = lax.broadcasted_iota(jnp.int32, (EXTRA, tok_count), 0)
    weight = jnp.concatenate(
        [
            jnp.where((m[0:1, :] == doc) & (m[1:2, :] == 1), 1.0, 0.0).astype(jnp.bfloat16)
            for m in marks
        ],
        axis=1,
    )
    row = lax.broadcasted_iota(jnp.int32, (width, FEAT), 0)
    col = lax.broadcasted_iota(jnp.int32, (width, FEAT), 1)
    for r, out in enumerate(outs):
        at = row - RANK * meta_ref[r]
        pick_x = jnp.where(at == lax.rem(col, RANK), 1.0, 0.0).astype(jnp.bfloat16)
        pick_g = jnp.where(at == col // RANK, 1.0, 0.0).astype(jnp.bfloat16)
        x_wide = jnp.dot(xp, pick_x, preferred_element_type=jnp.float32)
        g_wide = jnp.dot(gp, pick_g, preferred_element_type=jnp.float32)
        product = x_wide * g_wide
        high = product.astype(jnp.bfloat16)
        low = (product - high.astype(jnp.float32)).astype(jnp.bfloat16)
        both = jnp.dot(weight, high, preferred_element_type=jnp.float32)
        both = both + jnp.dot(weight, low, preferred_element_type=jnp.float32)
        out[...] = both[:DOCS]


def gradients(total, marks, line, modules):
    meta = jnp.stack([lax.rem(line + r, modules) for r in range(modules)]).astype(jnp.int32)
    return pl.pallas_call(
        gradient_kernel,
        in_specs=[pl.BlockSpec(memory_space=pltpu.SMEM)]
        + [pl.BlockSpec(memory_space=pltpu.VMEM)] * (1 + len(marks)),
        out_shape=[jax.ShapeDtypeStruct((DOCS, FEAT), jnp.float32)] * modules,
        compiler_params=vmem_params(),
        cost_estimate=pl.CostEstimate(
            flops=4 * modules * 256 * 128 * FEAT, bytes_accessed=4 * FEAT * 128, transcendentals=0
        ),
        name="gradients",
    )(meta, total, *marks)


def corner_richardson_kernel(total_rows, meta_ref, own, across, along, opp_a, opp_b, *refs):
    q_refs, (out_ref, pack_ref, full_ref) = refs[:-3], refs[-3:]
    pack_ref[meta_ref[0]] = own[:BLOCK]
    pack_ref[meta_ref[1]] = across[:BLOCK]
    pack_ref[meta_ref[2]] = along[:BLOCK]
    pack_ref[meta_ref[3], : BLOCK // 2] = opp_a[...]
    pack_ref[meta_ref[3], BLOCK // 2 :] = opp_b[: BLOCK // 2]
    packed = pack_ref[...].reshape(FEAT, HALF)
    at_row = lax.broadcasted_iota(jnp.int32, (HALF, HALF), 0)
    at_col = lax.broadcasted_iota(jnp.int32, (HALF, HALF), 1)
    both = packed[HALF:].astype(jnp.float32)
    both_t = both.T
    zero = jnp.zeros_like(both)
    above, below = at_row < at_col, at_row > at_col
    full_ref[:HALF, :HALF] = jnp.where(above, both, jnp.where(below, both_t, zero)).astype(jnp.bfloat16)
    full_ref[HALF:, HALF:] = jnp.where(below, both, jnp.where(above, both_t, zero)).astype(jnp.bfloat16)
    cross = packed[:HALF]
    full_ref[:HALF, HALF:] = cross
    full_ref[HALF:, :HALF] = cross.astype(jnp.float32).T.astype(jnp.bfloat16)
    diag = diag_of_rows(own[BLOCK:]) + diag_of_rows(across[BLOCK:])
    diag = diag + (diag_of_rows(along[BLOCK:]) + diag_of_rows(opp_b[BLOCK // 2 :]))
    diag = jnp.concatenate([diag[0:1], diag[1:2]], axis=1) / total_rows
    mean_diag = jnp.sum(diag, axis=1, keepdims=True) / FEAT
    step_size = 1.0 / (spread * (mean_diag + epsilon))
    own_diag = diag + damping * mean_diag
    lines = len(q_refs)
    queries = jnp.concatenate([q[...] for q in q_refs], axis=0)
    count = queries.shape[0]
    v = step_size * queries
    for _ in range(STEPS):
        high = v.astype(jnp.bfloat16)
        rest = v - high.astype(jnp.float32)
        mid = rest.astype(jnp.bfloat16)
        low = (rest - mid.astype(jnp.float32)).astype(jnp.bfloat16)
        parts = jnp.concatenate([high, mid, low], axis=0)
        off = jnp.dot(parts, full_ref[...], preferred_element_type=jnp.float32)
        off = off[:count] + (off[count : 2 * count] + off[2 * count :])
        v = v + step_size * (queries - (off / total_rows + own_diag * v))
    to = lax.broadcasted_iota(jnp.int32, (count, count), 0)
    at = lax.broadcasted_iota(jnp.int32, (count, count), 1)
    source = jnp.zeros((count, count), jnp.int32)
    for r in range(lines):
        here = (to >= DOCS * meta_ref[4 + r]) & (to < DOCS * (meta_ref[4 + r] + 1))
        source = jnp.where(here, to + DOCS * (r - meta_ref[4 + r]), source)
    order = jnp.where(at == source, 1.0, 0.0).astype(jnp.bfloat16)
    out_ref[...] = jnp.dot(order, v.astype(jnp.bfloat16), preferred_element_type=jnp.float32).astype(
        jnp.bfloat16
    )


def corner_precondition(total_rows, pieces, corner, line, queries):
    lines = len(queries)
    meta = jnp.stack(
        [corner ^ j for j in range(4)] + [lax.rem(line - r + lines, lines) for r in range(lines)]
    ).astype(jnp.int32)
    count = lines * DOCS
    return pl.pallas_call(
        functools.partial(corner_richardson_kernel, total_rows),
        in_specs=[pl.BlockSpec(memory_space=pltpu.SMEM)]
        + [pl.BlockSpec(memory_space=pltpu.VMEM)] * (5 + lines),
        out_shape=jax.ShapeDtypeStruct((count, FEAT), jnp.bfloat16),
        scratch_shapes=[
            pltpu.VMEM((4, BLOCK, HALF), jnp.bfloat16),
            pltpu.VMEM((FEAT, FEAT), jnp.bfloat16),
        ],
        compiler_params=vmem_params(),
        cost_estimate=pl.CostEstimate(
            flops=2 * STEPS * 3 * count * FEAT * FEAT, bytes_accessed=4 * FEAT * FEAT, transcendentals=0
        ),
        name="richardson",
    )(meta, *pieces, *queries)


def corner_score_kernel(scale, meta_ref, *refs):
    pieces, s_ref, mine_ref, other_ref, flat_ref = refs[:4], refs[4], refs[5], refs[6], refs[7]
    lines, count, _ = pieces[0].shape

    @pl.when(pl.program_id(0) == 0)
    def _():
        for j, piece in enumerate(pieces):
            at = pl.multiple_of(meta_ref[j] * count, count)
            for s in range(lines):
                col = pl.multiple_of(meta_ref[4 + s] * FEAT, FEAT)
                flat_ref[pl.ds(at, count), pl.ds(col, FEAT)] = piece[s]

    scores = lax.dot_general(
        s_ref[...], flat_ref[...], (((1,), (1,)), ((), ())), preferred_element_type=jnp.float32
    )
    scores = scale * scores.T
    rows = [
        scores[k * count + z * DOCS : k * count + (z + 1) * DOCS] for z in range(lines) for k in range(4)
    ]
    half = len(rows) // 2
    low, high = jnp.concatenate(rows[:half], axis=0), jnp.concatenate(rows[half:], axis=0)
    first = meta_ref[4 + lines] == 0
    mine_ref[...] = jnp.where(first, low, high)
    other_ref[...] = jnp.where(first, high, low)


def corner_score(pieces, stored, corner, line, scale):
    lines, count, _ = pieces[0].shape
    rows, width = stored.shape
    total = 4 * count
    tile = 512
    meta = jnp.stack(
        [corner ^ j for j in range(4)]
        + [lax.rem(line - s + lines, lines) for s in range(lines)]
        + [lax.axis_index("ctx")]
    ).astype(jnp.int32)
    shape = (total // 2, rows)
    return pl.pallas_call(
        functools.partial(corner_score_kernel, scale),
        grid_spec=pltpu.PrefetchScalarGridSpec(
            num_scalar_prefetch=1,
            grid=(rows // tile,),
            in_specs=[pl.BlockSpec(p.shape, lambda i, meta: (0, 0, 0)) for p in pieces]
            + [pl.BlockSpec((tile, width), lambda i, meta: (i, 0))],
            out_specs=[pl.BlockSpec((shape[0], tile), lambda i, meta: (0, i))] * 2,
            scratch_shapes=[pltpu.VMEM((total, width), jnp.bfloat16)],
        ),
        out_shape=[jax.ShapeDtypeStruct(shape, jnp.float32)] * 2,
        compiler_params=vmem_params(),
        cost_estimate=pl.CostEstimate(
            flops=2 * total * width * rows, bytes_accessed=2 * rows * width, transcendentals=0
        ),
        name="score",
    )(meta, *pieces, stored)


def to_corner(value, n_ex, bit):
    return lax.ppermute(value, "ex", [(e, e ^ bit) for e in range(n_ex)])


def to_plane(value, n_ex, shift):
    return lax.ppermute(value, "ex", [(e, (e + 4 * shift) % n_ex) for e in range(n_ex)])


def shards(acts, out_grads, projections, segments, valid, stored):
    n_ex = lax.axis_size("ex")
    n_ctx = lax.axis_size("ctx")
    mod_dev = projections.shape[2] // RANK
    if mod_dev != 4 or n_ex != 16 or n_ctx != 2:
        return general(acts, out_grads, projections, segments, valid, stored)
    lines = n_ex // 4
    tok_count = acts.shape[1]
    me = lax.axis_index("ex")
    line, corner = me // 4, lax.rem(me, 4)

    planes = {0: projections}
    for s in (1, 3, 2):
        planes[s] = to_plane(projections, n_ex, s)
    marks = swapped(jnp.concatenate([segments, valid], axis=0), n_ctx)
    across, along, opp0, opp1 = {}, {}, {}, {}
    order = [0, 1, 3, 2]
    grams = {}
    ties = []
    for i, s in enumerate(order):
        across[s] = to_corner(planes[s], n_ex, 1)
        along[s] = to_corner(planes[s], n_ex, 2)
        if i:
            p = order[i - 1]
            opp0[p] = to_corner(along[p][0], n_ex, 1)
            opp1[p] = to_corner(across[p][1], n_ex, 2)
        if i == 2:
            x_parts = swapped(acts[0], n_ctx)
        if i == 3:
            g_parts = swapped(out_grads[0], n_ctx)
        r = (i + 1) % lines
        grams[r] = block_gram(stored, lax.rem(line + r, lines), corner, ties)
        ties = [across[s], along[s]]
        if i:
            ties += [opp0[order[i - 1]], opp1[order[i - 1]]]
        if i < 3:
            ties += [planes[order[i + 1]]]
    last = order[-1]
    opp0[last] = to_corner(along[last][0], n_ex, 1)
    opp1[last] = to_corner(across[last][1], n_ex, 2)

    total = None
    for s in order:
        total = project(
            (planes[s], across[s], along[s], opp0[s], opp1[s]),
            x_parts,
            g_parts,
            lax.rem(line - s + lines, lines),
            corner,
            total,
        )
    docs = gradients(total, marks, line, mod_dev)
    queries = [docs[0]] + [to_plane(docs[s], n_ex, s) for s in range(1, lines)]

    sent = []
    for r in list(range(1, lines)) + [0]:
        o0, o1, o2, o3a, o3b, extra = grams[r]
        from_x = to_corner(o3a, n_ex, 1)
        from_y = to_corner(o3b, n_ex, 2)
        for_x, for_y = pass_on(o1, o2, from_x, from_y)
        got_x = to_corner(for_x, n_ex, 1)
        got_y = to_corner(for_y, n_ex, 2)
        if r:
            sent.append(to_plane(close(o0, got_x, got_y, extra), n_ex, r))
        else:
            kept = close(o0, got_x, got_y, extra, sent)

    kept_x = to_corner(kept, n_ex, 1)
    kept_y = to_corner(kept, n_ex, 2)
    opp_a = to_corner(kept_y[: BLOCK // 2], n_ex, 1)
    opp_b = to_corner(kept_x[BLOCK // 2 :], n_ex, 2)

    total_rows = stored.shape[0] * n_ex
    precond = corner_precondition(
        float(total_rows), (kept, kept_x, kept_y, opp_a, opp_b), corner, line, queries
    )

    stack = jnp.stack([precond] + [to_plane(precond, n_ex, s) for s in range(1, lines)])
    pieces = [stack] + [to_corner(stack, n_ex, bit) for bit in (1, 2, 3)]
    scale = 1.0 / math.sqrt(MODULES * FEAT * tok_count * n_ctx / DOCS)
    mine, other = corner_score(pieces, stored, corner, line, scale)
    return mine + lax.ppermute(other, "ctx", [(0, 1), (1, 0)])


def solution(mesh):
    in_specs = (
        P("ex", "ctx", None),
        P("ex", "ctx", None),
        P(None, "ex", "ctx"),
        P("ex", "ctx"),
        P("ex", "ctx"),
        P("ex", "ctx"),
    )
    out_specs = P("ctx", "ex")
    return jax.shard_map(shards, mesh=mesh, in_specs=in_specs, out_specs=out_specs, check_vma=False)
```

```python
import functools
import math

import jax
import jax.numpy as jnp
from jax import lax
from jax.experimental import pallas as pl
from jax.experimental.pallas import tpu as pltpu
from jax.sharding import PartitionSpec as P

RANK = 32
MODULES = 8
DOCS = 4
STEPS = 4
FEAT = RANK * RANK
HALF = FEAT // 2
BLOCK = FEAT // 4
EXTRA = 16

damping = 0.1
spread = 1.5
epsilon = 1e-06


def gram_kernel(s_ref, out_ref, diag_ref, ab_ref, c_ref):
    k = pl.program_id(1)

    @pl.when(k == 0)
    def _():
        ab_ref[...] = jnp.zeros_like(ab_ref)
        c_ref[...] = jnp.zeros_like(c_ref)

    rows = s_ref[...]
    contract = (((0,), (0,)), ((), ()))
    ab_ref[...] += lax.dot_general(
        rows[:, :HALF], rows, contract, preferred_element_type=jnp.float32
    )
    c_ref[...] += lax.dot_general(
        rows[:, HALF:], rows[:, HALF:], contract, preferred_element_type=jnp.float32
    )

    @pl.when(k == pl.num_programs(1) - 1)
    def _():
        at_row = lax.broadcasted_iota(jnp.int32, (HALF, HALF), 0)
        at_col = lax.broadcasted_iota(jnp.int32, (HALF, HALF), 1)
        a = ab_ref[:, :HALF]
        c = c_ref[...]
        out_ref[0, :HALF] = ab_ref[:, HALF:].astype(jnp.bfloat16)
        out_ref[0, HALF:] = jnp.where(at_row < at_col, a, c).astype(jnp.bfloat16)
        on = at_row == at_col
        diag_ref[0, :, :HALF] = jnp.sum(jnp.where(on, a, 0.0), axis=0, keepdims=True)
        diag_ref[0, :, HALF:] = jnp.sum(jnp.where(on, c, 0.0), axis=0, keepdims=True)


def packed_gram(stored):
    rows, cols = stored.shape
    modules = cols // FEAT
    depth = 1024
    while rows % depth:
        depth //= 2
    return pl.pallas_call(
        gram_kernel,
        grid=(modules, rows // depth),
        in_specs=[pl.BlockSpec((depth, FEAT), lambda m, k: (k, m))],
        out_specs=[
            pl.BlockSpec((1, FEAT, HALF), lambda m, k: (m, 0, 0)),
            pl.BlockSpec((1, 1, FEAT), lambda m, k: (m, 0, 0)),
        ],
        out_shape=[
            jax.ShapeDtypeStruct((modules, FEAT, HALF), jnp.bfloat16),
            jax.ShapeDtypeStruct((modules, 1, FEAT), jnp.float32),
        ],
        scratch_shapes=[
            pltpu.VMEM((HALF, FEAT), jnp.float32),
            pltpu.VMEM((HALF, HALF), jnp.float32),
        ],
        compiler_params=pltpu.CompilerParams(vmem_limit_bytes=32 * 1024 * 1024),
        cost_estimate=pl.CostEstimate(
            flops=2 * rows * FEAT * FEAT * modules * 3 // 4,
            bytes_accessed=rows * cols * 2 + modules * FEAT * HALF * 2,
            transcendentals=0,
        ),
        name="gram",
    )(stored)


def richardson_kernel(total_rows, packed_ref, diag_ref, q_ref, out_ref, full_ref):
    at_row = lax.broadcasted_iota(jnp.int32, (HALF, HALF), 0)
    at_col = lax.broadcasted_iota(jnp.int32, (HALF, HALF), 1)
    both = packed_ref[HALF:].astype(jnp.float32)
    both_t = both.T
    zero = jnp.zeros_like(both)
    above, below = at_row < at_col, at_row > at_col
    full_ref[:HALF, :HALF] = jnp.where(above, both, jnp.where(below, both_t, zero)).astype(jnp.bfloat16)
    full_ref[HALF:, HALF:] = jnp.where(below, both, jnp.where(above, both_t, zero)).astype(jnp.bfloat16)
    cross = packed_ref[:HALF]
    full_ref[:HALF, HALF:] = cross
    full_ref[HALF:, :HALF] = cross.astype(jnp.float32).T.astype(jnp.bfloat16)
    diag = diag_ref[...] / total_rows
    mean_diag = jnp.sum(diag, axis=1, keepdims=True) / FEAT
    step_size = 1.0 / (spread * (mean_diag + epsilon))
    own = diag + damping * mean_diag
    queries = q_ref[...]
    count = queries.shape[0]
    v = step_size * queries
    for _ in range(STEPS):
        high = v.astype(jnp.bfloat16)
        rest = v - high.astype(jnp.float32)
        mid = rest.astype(jnp.bfloat16)
        low = (rest - mid.astype(jnp.float32)).astype(jnp.bfloat16)
        parts = jnp.concatenate([high, mid, low], axis=0)
        off = jnp.dot(parts, full_ref[...], preferred_element_type=jnp.float32)
        off = off[:count] + (off[count : 2 * count] + off[2 * count :])
        v = v + step_size * (queries - (off / total_rows + own * v))
    out_ref[...] = v.astype(jnp.bfloat16)


def precondition(total_rows, packed, diag, queries):
    count = queries.shape[0]
    return pl.pallas_call(
        functools.partial(richardson_kernel, total_rows),
        out_shape=jax.ShapeDtypeStruct((count, FEAT), jnp.bfloat16),
        scratch_shapes=[pltpu.VMEM((FEAT, FEAT), jnp.bfloat16)],
        compiler_params=pltpu.CompilerParams(vmem_limit_bytes=32 * 1024 * 1024),
        cost_estimate=pl.CostEstimate(
            flops=2 * STEPS * 3 * count * FEAT * FEAT, bytes_accessed=4 * FEAT * FEAT, transcendentals=0
        ),
        name="richardson",
    )(packed, diag, queries)


def swapped(value, n_ctx):
    return [value] + [
        lax.ppermute(value, "ctx", [(i, (i + s) % n_ctx) for i in range(n_ctx)])
        for s in range(1, n_ctx)
    ]


def general(acts, out_grads, projections, segments, valid, stored):
    n_ex = lax.axis_size("ex")
    n_ctx = lax.axis_size("ctx")
    tok_count = acts.shape[1]
    mod_dev = projections.shape[2] // RANK
    owners = n_ex // mod_dev
    me = lax.axis_index("ex")

    weights = [lax.all_gather(projections[i], "ex", axis=0, tiled=True) for i in range(2)]
    x_parts = swapped(acts[0], n_ctx)
    g_parts = swapped(out_grads[0], n_ctx)
    marks = swapped(jnp.concatenate([segments, valid], axis=0), n_ctx)

    packed, diag = packed_gram(stored)
    sums = lax.psum_scatter(
        packed.reshape(n_ex, FEAT // owners, HALF), "ex", scatter_dimension=0, tiled=True
    )[0]
    diag = lax.psum(diag, "ex")
    groups = [list(range(m * owners, (m + 1) * owners)) for m in range(mod_dev)]
    packed_mine = lax.all_gather(sums, "ex", axis=0, tiled=True, axis_index_groups=groups)
    my_module = me // owners
    diag_mine = lax.dynamic_index_in_dim(diag, my_module, 0, keepdims=False)

    queries = 0.0
    doc_ids = jnp.arange(DOCS, dtype=jnp.int32)
    for x_rows, g_rows, mark in zip(x_parts, g_parts, marks):
        xp = jnp.dot(x_rows, weights[0], preferred_element_type=jnp.float32).astype(jnp.bfloat16)
        gp = jnp.dot(g_rows, weights[1], preferred_element_type=jnp.float32).astype(jnp.bfloat16)
        onehot = ((mark[0][None, :] == doc_ids[:, None]) & (mark[1][None, :] == 1)).astype(jnp.bfloat16)
        weighted = (onehot[:, :, None] * gp[None, :, :]).reshape(DOCS, tok_count, mod_dev, RANK)
        queries = queries + jnp.einsum(
            "qtmi,tmj->mqij",
            weighted,
            xp.reshape(tok_count, mod_dev, RANK),
            preferred_element_type=jnp.float32,
        )
    queries = queries.reshape(mod_dev, DOCS, FEAT)

    place = lax.rem(me, mod_dev)
    arrived = []
    for j in range(mod_dev):
        module = lax.rem(place + j, mod_dev)
        part = lax.dynamic_index_in_dim(queries, module, 0, keepdims=False)
        pairs = [
            (e, ((e % mod_dev + j) % mod_dev) * owners + e // mod_dev) for e in range(n_ex)
        ]
        arrived.append(lax.ppermute(part, "ex", pairs))
    arrived = jnp.stack(arrived)
    order = lax.rem(my_module - jnp.arange(mod_dev) + mod_dev, mod_dev)
    mine = jnp.take(arrived, order, axis=0).reshape(mod_dev * DOCS, FEAT)

    total_rows = stored.shape[0] * n_ex
    precond = precondition(float(total_rows), packed_mine, diag_mine, mine)

    flat = lax.all_gather(precond, "ex", axis=0, tiled=True).reshape(mod_dev, n_ex * DOCS, FEAT)
    flat = jnp.transpose(flat, (1, 0, 2)).reshape(n_ex * DOCS, mod_dev * FEAT)
    score_scale = 1.0 / math.sqrt(MODULES * FEAT * tok_count * n_ctx / DOCS)
    summed = lax.psum_scatter(
        lax.dot_general(flat, stored, (((1,), (1,)), ((), ())), preferred_element_type=jnp.float32),
        "ctx",
        scatter_dimension=0,
        tiled=True,
    )
    return summed * score_scale


def vmem_params(mib):
    return pltpu.CompilerParams(vmem_limit_bytes=mib * 1024 * 1024)


def small_cost(*arrays):
    return pl.CostEstimate(
        flops=0, bytes_accessed=sum(math.prod(a.shape) * a.dtype.itemsize for a in arrays), transcendentals=0
    )


def rows_of_diag(diag):
    high = diag.astype(jnp.bfloat16)
    rest = diag - high.astype(jnp.float32)
    mid = rest.astype(jnp.bfloat16)
    low = (rest - mid.astype(jnp.float32)).astype(jnp.bfloat16)
    empty = jnp.zeros((EXTRA - 3 * diag.shape[0], HALF), jnp.float32)
    terms = [t.astype(jnp.float32) for t in (high, mid, low)]
    return jnp.concatenate(terms + [empty], axis=0).astype(jnp.bfloat16)


def diag_of_rows(rows):
    terms = rows.astype(jnp.float32)
    return terms[0:2] + (terms[2:4] + terms[4:6])


def block_gram_kernel(ties, meta_ref, s_ref, *refs):
    o0, o1, o2, o3a, o3b, extra_ref, ab_ref, c_ref, pay_ref = refs[ties:]
    k = pl.program_id(1)

    @pl.when(k == 0)
    def _():
        ab_ref[...] = jnp.zeros_like(ab_ref)
        c_ref[...] = jnp.zeros_like(c_ref)

    rows = s_ref[...]
    contract = (((0,), (0,)), ((), ()))
    ab_ref[...] += lax.dot_general(
        rows[:, :HALF], rows, contract, preferred_element_type=jnp.float32
    )
    c_ref[...] += lax.dot_general(
        rows[:, HALF:], rows[:, HALF:], contract, preferred_element_type=jnp.float32
    )

    @pl.when(k == pl.num_programs(1) - 1)
    def _():
        at_row = lax.broadcasted_iota(jnp.int32, (HALF, HALF), 0)
        at_col = lax.broadcasted_iota(jnp.int32, (HALF, HALF), 1)
        a = ab_ref[:, :HALF]
        c = c_ref[...]
        cross = ab_ref[:, HALF:].astype(jnp.bfloat16)
        both = jnp.where(at_row < at_col, a, c).astype(jnp.bfloat16)
        pay_ref[0] = cross[:BLOCK]
        pay_ref[1] = cross[BLOCK:]
        pay_ref[2] = both[:BLOCK]
        pay_ref[3] = both[BLOCK:]
        on = at_row == at_col
        diag_a = jnp.sum(jnp.where(on, a, 0.0), axis=0, keepdims=True)
        diag_c = jnp.sum(jnp.where(on, c, 0.0), axis=0, keepdims=True)
        extra_ref[0] = rows_of_diag(jnp.concatenate([diag_a, diag_c], axis=0))
        o0[0] = pay_ref[meta_ref[2]]
        o1[0] = pay_ref[meta_ref[3]]
        o2[0] = pay_ref[meta_ref[4]]
        o3a[0] = pay_ref[meta_ref[5], : BLOCK // 2]
        o3b[0] = pay_ref[meta_ref[5], BLOCK // 2 :]


def block_gram(stored, modules, corner, ties):
    rows = stored.shape[0]
    depth = 1024
    while rows % depth:
        depth //= 2
    meta = jnp.stack(modules + [corner ^ j for j in range(4)]).astype(jnp.int32)
    heights = [BLOCK, BLOCK, BLOCK, BLOCK // 2, BLOCK // 2, EXTRA]
    count = len(modules)
    return pl.pallas_call(
        functools.partial(block_gram_kernel, len(ties)),
        grid_spec=pltpu.PrefetchScalarGridSpec(
            num_scalar_prefetch=1,
            grid=(count, rows // depth),
            in_specs=[pl.BlockSpec((depth, FEAT), lambda i, k, meta: (k, meta[i]))]
            + [pl.BlockSpec(memory_space=pl.ANY)] * len(ties),
            out_specs=[pl.BlockSpec((1, h, HALF), lambda i, k, meta: (i, 0, 0)) for h in heights],
            scratch_shapes=[
                pltpu.VMEM((HALF, FEAT), jnp.float32),
                pltpu.VMEM((HALF, HALF), jnp.float32),
                pltpu.VMEM((4, BLOCK, HALF), jnp.bfloat16),
            ],
        ),
        out_shape=[jax.ShapeDtypeStruct((count, h, HALF), jnp.bfloat16) for h in heights],
        compiler_params=vmem_params(16),
        cost_estimate=pl.CostEstimate(
            flops=2 * count * rows * FEAT * FEAT * 3 // 4,
            bytes_accessed=count * (rows * FEAT * 2 + FEAT * HALF * 2),
            transcendentals=0,
        ),
        name="gram",
    )(meta, pltpu.with_memory_space_constraint(stored, pltpu.HBM), *ties)


def side_kernel(count, *refs):
    out = refs[-1]
    for i in range(count):
        out[:, i] = refs[i][...]


def side_by_side(arrays, tie):
    whole = pl.BlockSpec(memory_space=pltpu.VMEM)
    first = arrays[0]
    return pl.pallas_call(
        functools.partial(side_kernel, len(arrays)),
        in_specs=[whole] * len(arrays) + [pl.BlockSpec(memory_space=pl.ANY)],
        out_shape=jax.ShapeDtypeStruct((first.shape[0], len(arrays)) + first.shape[1:], first.dtype),
        compiler_params=vmem_params(8),
        cost_estimate=small_cost(*arrays),
        name="side_by_side",
    )(*arrays, tie)


def forward_kernel(y0, yb, x0, xb, tie, for_x, for_y):
    for_x[0] = y0[0]
    for_x[1:] = yb[0]
    for_y[0] = x0[0]
    for_y[1:] = xb[0]


def forward(x0, xb, y0, yb, tie):
    depth, width = x0.shape[1:]
    count = xb.shape[1]
    out = jax.ShapeDtypeStruct((count + 1, depth, width), x0.dtype)

    def spec(shape, first):
        return pl.BlockSpec((1,) + shape[1:], lambda i: (first,) + (0,) * (len(shape) - 1))

    return pl.pallas_call(
        forward_kernel,
        grid=(1,),
        in_specs=[spec(y0.shape, 0), spec(yb.shape, 0), spec(x0.shape, 1), spec(xb.shape, 1)]
        + [pl.BlockSpec(memory_space=pl.ANY)],
        out_specs=[pl.BlockSpec(out.shape, lambda i: (0, 0, 0))] * 2,
        out_shape=[out] * 2,
        compiler_params=vmem_params(16),
        cost_estimate=small_cost(x0, xb),
        name="forward",
    )(y0, yb, x0, xb, tie)


def pass_kernel(o1, o2, from_x, from_y, *refs):
    for_x, for_y = refs[-2:]
    half = BLOCK // 2
    f32 = jnp.float32
    for_x[:, :half] = o1[:, :half]
    for_x[:, half:] = (o1[:, half:].astype(f32) + from_y[...].astype(f32)).astype(jnp.bfloat16)
    for_y[:, :half] = (o2[:, :half].astype(f32) + from_x[...].astype(f32)).astype(jnp.bfloat16)
    for_y[:, half:] = o2[:, half:]


def pass_on(o1, o2, from_x, from_y, ties=()):
    return pl.pallas_call(
        pass_kernel,
        in_specs=[pl.BlockSpec(memory_space=pltpu.VMEM)] * 4
        + [pl.BlockSpec(memory_space=pl.ANY)] * len(ties),
        out_shape=[jax.ShapeDtypeStruct(o1.shape, o1.dtype)] * 2,
        compiler_params=vmem_params(8),
        cost_estimate=small_cost(o1, o2, o1, o2),
        name="pass_on",
    )(o1, o2, from_x, from_y, *ties)


def close_kernel(slots, count, o0, got_x, got_y, extra, *refs):
    arrived, outs = refs[:count], refs[-len(slots) :]
    f32 = jnp.float32
    for i, out in zip(slots, outs):
        total = o0[i].astype(f32) + got_x[i].astype(f32) + got_y[i].astype(f32)
        if not count:
            out[:BLOCK] = total.astype(jnp.bfloat16)
            out[BLOCK:] = extra[i]
            continue
        diag = diag_of_rows(extra[i])
        for other in arrived:
            total = total + other[:BLOCK].astype(f32)
            diag = diag + diag_of_rows(other[BLOCK:])
        out[:BLOCK] = total.astype(jnp.bfloat16)
        out[BLOCK:] = rows_of_diag(diag)


def close(o0, got_x, got_y, extra, slots, arrived=(), ties=()):
    return pl.pallas_call(
        functools.partial(close_kernel, slots, len(arrived)),
        in_specs=[pl.BlockSpec(memory_space=pltpu.VMEM)] * (4 + len(arrived))
        + [pl.BlockSpec(memory_space=pl.ANY)] * len(ties),
        out_shape=[jax.ShapeDtypeStruct((BLOCK + EXTRA, HALF), jnp.bfloat16)] * len(slots),
        compiler_params=vmem_params(8),
        cost_estimate=small_cost(o0, got_x, got_y, *arrived),
        name="close",
    )(o0, got_x, got_y, extra, *arrived, *ties)


def project_kernel(meta_ref, own0, own_b, x0, xb, y0, yb, opp_x, opp_y, *refs):
    rest, out = refs[:-1], refs[-1]
    parts = len(rest) // 2
    depth = own0.shape[1]
    for which in range(2):
        weights = []
        for r0, rb in ((own0, own_b), (x0, xb), (y0, yb)):
            weights.append([r0.at[which]] + [rb.at[which, i] for i in range(3)])
        opp = (opp_x, opp_y)[which]
        weights.append([opp.at[i] for i in range(4)])
        for part in range(parts):
            rows = rest[which * parts + part]
            total = None
            for corner in range(4):
                for i in range(4):
                    at = pl.multiple_of(meta_ref[corner * 4 + i] * depth, depth)
                    term = jnp.dot(
                        rows[:, pl.ds(at, depth)],
                        weights[corner][i][...],
                        preferred_element_type=jnp.float32,
                    )
                    total = term if total is None else total + term
            out[which, part] = total


def project(pieces, x_parts, g_parts, planes, corner):
    width = pieces[0].shape[-1]
    tok_count = x_parts[0].shape[0]
    meta = jnp.stack([4 * p + (corner ^ j) for j in range(4) for p in planes]).astype(jnp.int32)
    depth = pieces[0].shape[1]
    return pl.pallas_call(
        project_kernel,
        in_specs=[pl.BlockSpec(memory_space=pltpu.SMEM)]
        + [pl.BlockSpec(memory_space=pltpu.VMEM)] * (len(pieces) + 2 * len(x_parts)),
        out_shape=jax.ShapeDtypeStruct((2, len(x_parts), tok_count, width), jnp.float32),
        compiler_params=vmem_params(24),
        cost_estimate=pl.CostEstimate(
            flops=2 * 2 * len(x_parts) * tok_count * 16 * depth * width,
            bytes_accessed=2 * (2 * len(x_parts) * tok_count + 2 * width) * 16 * depth,
            transcendentals=0,
        ),
        name="project",
    )(meta, *pieces, *x_parts, *g_parts)


def gradient_kernel(meta_ref, total_ref, *refs):
    parts = total_ref.shape[1]
    marks, outs = refs[:parts], refs[parts:]
    width = total_ref.shape[3]
    xp = jnp.concatenate([total_ref[0, p].astype(jnp.bfloat16) for p in range(parts)], axis=0)
    gp = jnp.concatenate([total_ref[1, p].astype(jnp.bfloat16) for p in range(parts)], axis=0)
    tok_count = total_ref.shape[2]
    doc = lax.broadcasted_iota(jnp.int32, (EXTRA, tok_count), 0)
    weight = jnp.concatenate(
        [
            jnp.where((m[0:1, :] == doc) & (m[1:2, :] == 1), 1.0, 0.0).astype(jnp.bfloat16)
            for m in marks
        ],
        axis=1,
    )
    row = lax.broadcasted_iota(jnp.int32, (width, FEAT), 0)
    col = lax.broadcasted_iota(jnp.int32, (width, FEAT), 1)
    for r, out in enumerate(outs):
        at = row - RANK * meta_ref[r]
        pick_x = jnp.where(at == lax.rem(col, RANK), 1.0, 0.0).astype(jnp.bfloat16)
        pick_g = jnp.where(at == col // RANK, 1.0, 0.0).astype(jnp.bfloat16)
        x_wide = jnp.dot(xp, pick_x, preferred_element_type=jnp.float32)
        g_wide = jnp.dot(gp, pick_g, preferred_element_type=jnp.float32)
        product = x_wide * g_wide
        high = product.astype(jnp.bfloat16)
        low = (product - high.astype(jnp.float32)).astype(jnp.bfloat16)
        both = jnp.dot(weight, high, preferred_element_type=jnp.float32)
        both = both + jnp.dot(weight, low, preferred_element_type=jnp.float32)
        out[...] = both[:DOCS]


def gradients(total, marks, line, modules):
    meta = jnp.stack([lax.rem(line + r, modules) for r in range(modules)]).astype(jnp.int32)
    return pl.pallas_call(
        gradient_kernel,
        in_specs=[pl.BlockSpec(memory_space=pltpu.SMEM)]
        + [pl.BlockSpec(memory_space=pltpu.VMEM)] * (1 + len(marks)),
        out_shape=[jax.ShapeDtypeStruct((DOCS, FEAT), jnp.float32)] * modules,
        compiler_params=vmem_params(16),
        cost_estimate=pl.CostEstimate(
            flops=4 * modules * 256 * 128 * FEAT, bytes_accessed=4 * FEAT * 128, transcendentals=0
        ),
        name="gradients",
    )(meta, total, *marks)


def corner_richardson_kernel(total_rows, meta_ref, own, across, along, opp_a, opp_b, *refs):
    q_refs, (out_ref, pack_ref, full_ref) = refs[:-3], refs[-3:]
    pack_ref[meta_ref[0]] = own[:BLOCK]
    pack_ref[meta_ref[1]] = across[:BLOCK]
    pack_ref[meta_ref[2]] = along[:BLOCK]
    pack_ref[meta_ref[3], : BLOCK // 2] = opp_a[...]
    pack_ref[meta_ref[3], BLOCK // 2 :] = opp_b[: BLOCK // 2]
    packed = pack_ref[...].reshape(FEAT, HALF)
    at_row = lax.broadcasted_iota(jnp.int32, (HALF, HALF), 0)
    at_col = lax.broadcasted_iota(jnp.int32, (HALF, HALF), 1)
    both = packed[HALF:].astype(jnp.float32)
    both_t = both.T
    zero = jnp.zeros_like(both)
    above, below = at_row < at_col, at_row > at_col
    full_ref[:HALF, :HALF] = jnp.where(above, both, jnp.where(below, both_t, zero)).astype(jnp.bfloat16)
    full_ref[HALF:, HALF:] = jnp.where(below, both, jnp.where(above, both_t, zero)).astype(jnp.bfloat16)
    cross = packed[:HALF]
    full_ref[:HALF, HALF:] = cross
    full_ref[HALF:, :HALF] = cross.astype(jnp.float32).T.astype(jnp.bfloat16)
    diag = diag_of_rows(own[BLOCK:]) + diag_of_rows(across[BLOCK:])
    diag = diag + (diag_of_rows(along[BLOCK:]) + diag_of_rows(opp_b[BLOCK // 2 :]))
    diag = jnp.concatenate([diag[0:1], diag[1:2]], axis=1) / total_rows
    mean_diag = jnp.sum(diag, axis=1, keepdims=True) / FEAT
    step_size = 1.0 / (spread * (mean_diag + epsilon))
    own_diag = diag + damping * mean_diag
    lines = len(q_refs)
    queries = jnp.concatenate([q[...] for q in q_refs], axis=0)
    count = queries.shape[0]
    v = step_size * queries
    for _ in range(STEPS):
        high = v.astype(jnp.bfloat16)
        rest = v - high.astype(jnp.float32)
        mid = rest.astype(jnp.bfloat16)
        low = (rest - mid.astype(jnp.float32)).astype(jnp.bfloat16)
        parts = jnp.concatenate([high, mid, low], axis=0)
        off = jnp.dot(parts, full_ref[...], preferred_element_type=jnp.float32)
        off = off[:count] + (off[count : 2 * count] + off[2 * count :])
        v = v + step_size * (queries - (off / total_rows + own_diag * v))
    to = lax.broadcasted_iota(jnp.int32, (count, count), 0)
    at = lax.broadcasted_iota(jnp.int32, (count, count), 1)
    source = jnp.zeros((count, count), jnp.int32)
    for r in range(lines):
        here = (to >= DOCS * meta_ref[4 + r]) & (to < DOCS * (meta_ref[4 + r] + 1))
        source = jnp.where(here, to + DOCS * (r - meta_ref[4 + r]), source)
    order = jnp.where(at == source, 1.0, 0.0).astype(jnp.bfloat16)
    out_ref[...] = jnp.dot(order, v.astype(jnp.bfloat16), preferred_element_type=jnp.float32).astype(
        jnp.bfloat16
    )


def corner_precondition(total_rows, pieces, corner, line, queries):
    lines = len(queries)
    meta = jnp.stack(
        [corner ^ j for j in range(4)] + [lax.rem(line - r + lines, lines) for r in range(lines)]
    ).astype(jnp.int32)
    count = lines * DOCS
    return pl.pallas_call(
        functools.partial(corner_richardson_kernel, total_rows),
        in_specs=[pl.BlockSpec(memory_space=pltpu.SMEM)]
        + [pl.BlockSpec(memory_space=pltpu.VMEM)] * (5 + lines),
        out_shape=jax.ShapeDtypeStruct((count, FEAT), jnp.bfloat16),
        scratch_shapes=[
            pltpu.VMEM((4, BLOCK, HALF), jnp.bfloat16),
            pltpu.VMEM((FEAT, FEAT), jnp.bfloat16),
        ],
        compiler_params=vmem_params(16),
        cost_estimate=pl.CostEstimate(
            flops=2 * STEPS * 3 * count * FEAT * FEAT, bytes_accessed=4 * FEAT * FEAT, transcendentals=0
        ),
        name="richardson",
    )(meta, *pieces, *queries)


def corner_score_kernel(scale, meta_ref, *refs):
    pieces, s_ref, mine_ref, other_ref, flat_ref = refs[:4], refs[4], refs[5], refs[6], refs[7]
    lines, count, _ = pieces[0].shape

    @pl.when(pl.program_id(0) == 0)
    def _():
        for j, piece in enumerate(pieces):
            at = pl.multiple_of(meta_ref[j] * count, count)
            for s in range(lines):
                col = pl.multiple_of(meta_ref[4 + s] * FEAT, FEAT)
                flat_ref[pl.ds(at, count), pl.ds(col, FEAT)] = piece[s]

    scores = lax.dot_general(
        s_ref[...], flat_ref[...], (((1,), (1,)), ((), ())), preferred_element_type=jnp.float32
    )
    scores = scale * scores.T
    rows = [
        scores[k * count + z * DOCS : k * count + (z + 1) * DOCS] for z in range(lines) for k in range(4)
    ]
    half = len(rows) // 2
    low, high = jnp.concatenate(rows[:half], axis=0), jnp.concatenate(rows[half:], axis=0)
    first = meta_ref[4 + lines] == 0
    mine_ref[...] = jnp.where(first, low, high)
    other_ref[...] = jnp.where(first, high, low)


def corner_score(pieces, stored, corner, line, scale):
    lines, count, _ = pieces[0].shape
    rows, width = stored.shape
    total = 4 * count
    tile = 256
    meta = jnp.stack(
        [corner ^ j for j in range(4)]
        + [lax.rem(line - s + lines, lines) for s in range(lines)]
        + [lax.axis_index("ctx")]
    ).astype(jnp.int32)
    shape = (total // 2, rows)
    return pl.pallas_call(
        functools.partial(corner_score_kernel, scale),
        grid_spec=pltpu.PrefetchScalarGridSpec(
            num_scalar_prefetch=1,
            grid=(rows // tile,),
            in_specs=[pl.BlockSpec(p.shape, lambda i, meta: (0, 0, 0)) for p in pieces]
            + [pl.BlockSpec((tile, width), lambda i, meta: (i, 0))],
            out_specs=[pl.BlockSpec((shape[0], tile), lambda i, meta: (0, i))] * 2,
            scratch_shapes=[pltpu.VMEM((total, width), jnp.bfloat16)],
        ),
        out_shape=[jax.ShapeDtypeStruct(shape, jnp.float32)] * 2,
        compiler_params=vmem_params(24),
        cost_estimate=pl.CostEstimate(
            flops=2 * total * width * rows, bytes_accessed=2 * rows * width, transcendentals=0
        ),
        name="score",
    )(meta, *pieces, pltpu.with_memory_space_constraint(stored, pltpu.HBM))


def to_corner(value, n_ex, bit):
    return lax.ppermute(value, "ex", [(e, e ^ bit) for e in range(n_ex)])


def to_plane(value, n_ex, shift):
    return lax.ppermute(value, "ex", [(e, (e + 4 * shift) % n_ex) for e in range(n_ex)])


def shards(acts, out_grads, projections, segments, valid, stored):
    n_ex = lax.axis_size("ex")
    n_ctx = lax.axis_size("ctx")
    mod_dev = projections.shape[2] // RANK
    if mod_dev != 4 or n_ex != 16 or n_ctx != 2:
        return general(acts, out_grads, projections, segments, valid, stored)
    lines = n_ex // 4
    tok_count = acts.shape[1]
    me = lax.axis_index("ex")
    line, corner = me // 4, lax.rem(me, 4)

    def gram(planes, ties):
        return block_gram(stored, [lax.rem(line + r, lines) for r in planes], corner, ties)

    line1, line3, line2 = (to_plane(projections, n_ex, s) for s in (1, 3, 2))
    x0, y0 = to_corner(projections, n_ex, 1), to_corner(projections, n_ex, 2)
    o0, o1, o2, o3a, o3b, extra = gram((1, 2), [])
    own_b = side_by_side([line1, line3, line2], extra)
    from_x, from_y = to_corner(o3a, n_ex, 1), to_corner(o3b, n_ex, 2)
    xb, yb = to_corner(own_b, n_ex, 1), to_corner(own_b, n_ex, 2)
    p0, p1, p2, p3a, p3b, extra_b = gram((3, 0), [own_b, x0, y0])
    x_parts = swapped(acts[0], n_ctx)
    g_parts = swapped(out_grads[0], n_ctx)
    marks = swapped(jnp.concatenate([segments, valid], axis=0), n_ctx)
    for_x, for_y = pass_on(o1, o2, from_x, from_y, (extra_b, x_parts[1], g_parts[1]))
    got_x, got_y = to_corner(for_x, n_ex, 1), to_corner(for_y, n_ex, 2)
    from_xb, from_yb = to_corner(p3a, n_ex, 1), to_corner(p3b, n_ex, 2)
    opp_x, opp_y = forward(x0, xb, y0, yb, for_x)
    opp_x, opp_y = to_corner(opp_x, n_ex, 1), to_corner(opp_y, n_ex, 2)

    planes = [lax.rem(line - s + lines, lines) for s in (0, 1, 3, 2)]
    total = project((projections, own_b, x0, xb, y0, yb, opp_x, opp_y), x_parts, g_parts, planes, corner)
    docs = gradients(total, marks, line, mod_dev)
    queries = [docs[0]] + [to_plane(docs[s], n_ex, s) for s in range(1, lines)]

    message1, message2 = close(o0, got_x, got_y, extra, (0, 1))
    for_xb, for_yb = pass_on(p1, p2, from_xb, from_yb, (got_x, got_y))
    got_xb, got_yb = to_corner(for_xb, n_ex, 1), to_corner(for_yb, n_ex, 2)
    sent = [to_plane(message1, n_ex, 1), to_plane(message2, n_ex, 2)]
    (message3,) = close(p0, got_xb, got_yb, extra_b, (0,), (), (docs[0],))
    sent.append(to_plane(message3, n_ex, 3))
    (kept,) = close(p0, got_xb, got_yb, extra_b, (1,), sent, queries[1:])

    kept_x, kept_y = to_corner(kept, n_ex, 1), to_corner(kept, n_ex, 2)
    opp_a = to_corner(kept_y[: BLOCK // 2], n_ex, 1)
    opp_b = to_corner(kept_x[BLOCK // 2 :], n_ex, 2)

    total_rows = stored.shape[0] * n_ex
    precond = corner_precondition(
        float(total_rows), (kept, kept_x, kept_y, opp_a, opp_b), corner, line, queries
    )

    stack = jnp.stack([precond] + [to_plane(precond, n_ex, s) for s in range(1, lines)])
    pieces = [stack] + [to_corner(stack, n_ex, bit) for bit in (1, 2, 3)]
    scale = 1.0 / math.sqrt(MODULES * FEAT * tok_count * n_ctx / DOCS)
    mine, other = corner_score(pieces, stored, corner, line, scale)
    return mine + lax.ppermute(other, "ctx", [(0, 1), (1, 0)])


def solution(mesh):
    in_specs = (
        P("ex", "ctx", None),
        P("ex", "ctx", None),
        P(None, "ex", "ctx"),
        P("ex", "ctx"),
        P("ex", "ctx"),
        P("ex", "ctx"),
    )
    out_specs = P("ctx", "ex")
    return jax.shard_map(shards, mesh=mesh, in_specs=in_specs, out_specs=out_specs, check_vma=False)
```

```python
import functools
import math

import jax
import jax.numpy as jnp
from jax import lax
from jax.experimental import pallas as pl
from jax.experimental.pallas import tpu as pltpu
from jax.sharding import PartitionSpec as P

RANK = 32
MODULES = 8
DOCS = 4
STEPS = 4
FEAT = RANK * RANK
HALF = FEAT // 2
BLOCK = FEAT // 4
EXTRA = 16

damping = 0.1
spread = 1.5
epsilon = 1e-06


def gram_kernel(s_ref, out_ref, diag_ref, ab_ref, c_ref):
    k = pl.program_id(1)

    @pl.when(k == 0)
    def _():
        ab_ref[...] = jnp.zeros_like(ab_ref)
        c_ref[...] = jnp.zeros_like(c_ref)

    rows = s_ref[...]
    contract = (((0,), (0,)), ((), ()))
    ab_ref[...] += lax.dot_general(
        rows[:, :HALF], rows, contract, preferred_element_type=jnp.float32
    )
    c_ref[...] += lax.dot_general(
        rows[:, HALF:], rows[:, HALF:], contract, preferred_element_type=jnp.float32
    )

    @pl.when(k == pl.num_programs(1) - 1)
    def _():
        at_row = lax.broadcasted_iota(jnp.int32, (HALF, HALF), 0)
        at_col = lax.broadcasted_iota(jnp.int32, (HALF, HALF), 1)
        a = ab_ref[:, :HALF]
        c = c_ref[...]
        out_ref[0, :HALF] = ab_ref[:, HALF:].astype(jnp.bfloat16)
        out_ref[0, HALF:] = jnp.where(at_row < at_col, a, c).astype(jnp.bfloat16)
        on = at_row == at_col
        diag_ref[0, :, :HALF] = jnp.sum(jnp.where(on, a, 0.0), axis=0, keepdims=True)
        diag_ref[0, :, HALF:] = jnp.sum(jnp.where(on, c, 0.0), axis=0, keepdims=True)


def packed_gram(stored):
    rows, cols = stored.shape
    modules = cols // FEAT
    depth = 1024
    while rows % depth:
        depth //= 2
    return pl.pallas_call(
        gram_kernel,
        grid=(modules, rows // depth),
        in_specs=[pl.BlockSpec((depth, FEAT), lambda m, k: (k, m))],
        out_specs=[
            pl.BlockSpec((1, FEAT, HALF), lambda m, k: (m, 0, 0)),
            pl.BlockSpec((1, 1, FEAT), lambda m, k: (m, 0, 0)),
        ],
        out_shape=[
            jax.ShapeDtypeStruct((modules, FEAT, HALF), jnp.bfloat16),
            jax.ShapeDtypeStruct((modules, 1, FEAT), jnp.float32),
        ],
        scratch_shapes=[
            pltpu.VMEM((HALF, FEAT), jnp.float32),
            pltpu.VMEM((HALF, HALF), jnp.float32),
        ],
        compiler_params=pltpu.CompilerParams(vmem_limit_bytes=32 * 1024 * 1024),
        cost_estimate=pl.CostEstimate(
            flops=2 * rows * FEAT * FEAT * modules * 3 // 4,
            bytes_accessed=rows * cols * 2 + modules * FEAT * HALF * 2,
            transcendentals=0,
        ),
        name="gram",
    )(stored)


def richardson_kernel(total_rows, packed_ref, diag_ref, q_ref, out_ref, full_ref):
    at_row = lax.broadcasted_iota(jnp.int32, (HALF, HALF), 0)
    at_col = lax.broadcasted_iota(jnp.int32, (HALF, HALF), 1)
    both = packed_ref[HALF:].astype(jnp.float32)
    both_t = both.T
    zero = jnp.zeros_like(both)
    above, below = at_row < at_col, at_row > at_col
    full_ref[:HALF, :HALF] = jnp.where(above, both, jnp.where(below, both_t, zero)).astype(jnp.bfloat16)
    full_ref[HALF:, HALF:] = jnp.where(below, both, jnp.where(above, both_t, zero)).astype(jnp.bfloat16)
    cross = packed_ref[:HALF]
    full_ref[:HALF, HALF:] = cross
    full_ref[HALF:, :HALF] = cross.astype(jnp.float32).T.astype(jnp.bfloat16)
    diag = diag_ref[...] / total_rows
    mean_diag = jnp.sum(diag, axis=1, keepdims=True) / FEAT
    step_size = 1.0 / (spread * (mean_diag + epsilon))
    own = diag + damping * mean_diag
    queries = q_ref[...]
    count = queries.shape[0]
    v = step_size * queries
    for _ in range(STEPS):
        high = v.astype(jnp.bfloat16)
        rest = v - high.astype(jnp.float32)
        mid = rest.astype(jnp.bfloat16)
        low = (rest - mid.astype(jnp.float32)).astype(jnp.bfloat16)
        parts = jnp.concatenate([high, mid, low], axis=0)
        off = jnp.dot(parts, full_ref[...], preferred_element_type=jnp.float32)
        off = off[:count] + (off[count : 2 * count] + off[2 * count :])
        v = v + step_size * (queries - (off / total_rows + own * v))
    out_ref[...] = v.astype(jnp.bfloat16)


def precondition(total_rows, packed, diag, queries):
    count = queries.shape[0]
    return pl.pallas_call(
        functools.partial(richardson_kernel, total_rows),
        out_shape=jax.ShapeDtypeStruct((count, FEAT), jnp.bfloat16),
        scratch_shapes=[pltpu.VMEM((FEAT, FEAT), jnp.bfloat16)],
        compiler_params=pltpu.CompilerParams(vmem_limit_bytes=32 * 1024 * 1024),
        cost_estimate=pl.CostEstimate(
            flops=2 * STEPS * 3 * count * FEAT * FEAT, bytes_accessed=4 * FEAT * FEAT, transcendentals=0
        ),
        name="richardson",
    )(packed, diag, queries)


def swapped(value, n_ctx):
    return [value] + [
        lax.ppermute(value, "ctx", [(i, (i + s) % n_ctx) for i in range(n_ctx)])
        for s in range(1, n_ctx)
    ]


def general(acts, out_grads, projections, segments, valid, stored):
    n_ex = lax.axis_size("ex")
    n_ctx = lax.axis_size("ctx")
    tok_count = acts.shape[1]
    mod_dev = projections.shape[2] // RANK
    owners = n_ex // mod_dev
    me = lax.axis_index("ex")

    weights = [lax.all_gather(projections[i], "ex", axis=0, tiled=True) for i in range(2)]
    x_parts = swapped(acts[0], n_ctx)
    g_parts = swapped(out_grads[0], n_ctx)
    marks = swapped(jnp.concatenate([segments, valid], axis=0), n_ctx)

    packed, diag = packed_gram(stored)
    sums = lax.psum_scatter(
        packed.reshape(n_ex, FEAT // owners, HALF), "ex", scatter_dimension=0, tiled=True
    )[0]
    diag = lax.psum(diag, "ex")
    groups = [list(range(m * owners, (m + 1) * owners)) for m in range(mod_dev)]
    packed_mine = lax.all_gather(sums, "ex", axis=0, tiled=True, axis_index_groups=groups)
    my_module = me // owners
    diag_mine = lax.dynamic_index_in_dim(diag, my_module, 0, keepdims=False)

    queries = 0.0
    doc_ids = jnp.arange(DOCS, dtype=jnp.int32)
    for x_rows, g_rows, mark in zip(x_parts, g_parts, marks):
        xp = jnp.dot(x_rows, weights[0], preferred_element_type=jnp.float32).astype(jnp.bfloat16)
        gp = jnp.dot(g_rows, weights[1], preferred_element_type=jnp.float32).astype(jnp.bfloat16)
        onehot = ((mark[0][None, :] == doc_ids[:, None]) & (mark[1][None, :] == 1)).astype(jnp.bfloat16)
        weighted = (onehot[:, :, None] * gp[None, :, :]).reshape(DOCS, tok_count, mod_dev, RANK)
        queries = queries + jnp.einsum(
            "qtmi,tmj->mqij",
            weighted,
            xp.reshape(tok_count, mod_dev, RANK),
            preferred_element_type=jnp.float32,
        )
    queries = queries.reshape(mod_dev, DOCS, FEAT)

    place = lax.rem(me, mod_dev)
    arrived = []
    for j in range(mod_dev):
        module = lax.rem(place + j, mod_dev)
        part = lax.dynamic_index_in_dim(queries, module, 0, keepdims=False)
        pairs = [
            (e, ((e % mod_dev + j) % mod_dev) * owners + e // mod_dev) for e in range(n_ex)
        ]
        arrived.append(lax.ppermute(part, "ex", pairs))
    arrived = jnp.stack(arrived)
    order = lax.rem(my_module - jnp.arange(mod_dev) + mod_dev, mod_dev)
    mine = jnp.take(arrived, order, axis=0).reshape(mod_dev * DOCS, FEAT)

    total_rows = stored.shape[0] * n_ex
    precond = precondition(float(total_rows), packed_mine, diag_mine, mine)

    flat = lax.all_gather(precond, "ex", axis=0, tiled=True).reshape(mod_dev, n_ex * DOCS, FEAT)
    flat = jnp.transpose(flat, (1, 0, 2)).reshape(n_ex * DOCS, mod_dev * FEAT)
    score_scale = 1.0 / math.sqrt(MODULES * FEAT * tok_count * n_ctx / DOCS)
    summed = lax.psum_scatter(
        lax.dot_general(flat, stored, (((1,), (1,)), ((), ())), preferred_element_type=jnp.float32),
        "ctx",
        scatter_dimension=0,
        tiled=True,
    )
    return summed * score_scale


def vmem_params(mib):
    return pltpu.CompilerParams(vmem_limit_bytes=mib * 1024 * 1024)


def small_cost(*arrays):
    return pl.CostEstimate(
        flops=0, bytes_accessed=sum(math.prod(a.shape) * a.dtype.itemsize for a in arrays), transcendentals=0
    )


def rows_of_diag(diag):
    high = diag.astype(jnp.bfloat16)
    rest = diag - high.astype(jnp.float32)
    mid = rest.astype(jnp.bfloat16)
    low = (rest - mid.astype(jnp.float32)).astype(jnp.bfloat16)
    empty = jnp.zeros((EXTRA - 3 * diag.shape[0], HALF), jnp.float32)
    terms = [t.astype(jnp.float32) for t in (high, mid, low)]
    return jnp.concatenate(terms + [empty], axis=0).astype(jnp.bfloat16)


def diag_of_rows(rows):
    terms = rows.astype(jnp.float32)
    return terms[0:2] + (terms[2:4] + terms[4:6])


def block_gram_kernel(ties, meta_ref, s_ref, *refs):
    o0, o1, o2, o3a, o3b, extra_ref, ab_ref, c_ref, pay_ref = refs[ties:]
    k = pl.program_id(1)

    @pl.when(k == 0)
    def _():
        ab_ref[...] = jnp.zeros_like(ab_ref)
        c_ref[...] = jnp.zeros_like(c_ref)

    rows = s_ref[...]
    contract = (((0,), (0,)), ((), ()))
    ab_ref[...] += lax.dot_general(
        rows[:, :HALF], rows, contract, preferred_element_type=jnp.float32
    )
    c_ref[...] += lax.dot_general(
        rows[:, HALF:], rows[:, HALF:], contract, preferred_element_type=jnp.float32
    )

    @pl.when(k == pl.num_programs(1) - 1)
    def _():
        at_row = lax.broadcasted_iota(jnp.int32, (HALF, HALF), 0)
        at_col = lax.broadcasted_iota(jnp.int32, (HALF, HALF), 1)
        a = ab_ref[:, :HALF]
        c = c_ref[...]
        cross = ab_ref[:, HALF:].astype(jnp.bfloat16)
        both = jnp.where(at_row < at_col, a, c).astype(jnp.bfloat16)
        pay_ref[0] = cross[:BLOCK]
        pay_ref[1] = cross[BLOCK:]
        pay_ref[2] = both[:BLOCK]
        pay_ref[3] = both[BLOCK:]
        on = at_row == at_col
        diag_a = jnp.sum(jnp.where(on, a, 0.0), axis=0, keepdims=True)
        diag_c = jnp.sum(jnp.where(on, c, 0.0), axis=0, keepdims=True)
        extra_ref[0] = rows_of_diag(jnp.concatenate([diag_a, diag_c], axis=0))
        o0[0] = pay_ref[meta_ref[2]]
        o1[0] = pay_ref[meta_ref[3]]
        o2[0] = pay_ref[meta_ref[4]]
        o3a[0] = pay_ref[meta_ref[5], : BLOCK // 2]
        o3b[0] = pay_ref[meta_ref[5], BLOCK // 2 :]


def block_gram(stored, modules, corner, ties):
    rows = stored.shape[0]
    depth = 1024
    while rows % depth:
        depth //= 2
    meta = jnp.stack(modules + [corner ^ j for j in range(4)]).astype(jnp.int32)
    heights = [BLOCK, BLOCK, BLOCK, BLOCK // 2, BLOCK // 2, EXTRA]
    count = len(modules)
    return pl.pallas_call(
        functools.partial(block_gram_kernel, len(ties)),
        grid_spec=pltpu.PrefetchScalarGridSpec(
            num_scalar_prefetch=1,
            grid=(count, rows // depth),
            in_specs=[pl.BlockSpec((depth, FEAT), lambda i, k, meta: (k, meta[i]))]
            + [pl.BlockSpec(memory_space=pl.ANY)] * len(ties),
            out_specs=[pl.BlockSpec((1, h, HALF), lambda i, k, meta: (i, 0, 0)) for h in heights],
            scratch_shapes=[
                pltpu.VMEM((HALF, FEAT), jnp.float32),
                pltpu.VMEM((HALF, HALF), jnp.float32),
                pltpu.VMEM((4, BLOCK, HALF), jnp.bfloat16),
            ],
        ),
        out_shape=[jax.ShapeDtypeStruct((count, h, HALF), jnp.bfloat16) for h in heights],
        compiler_params=vmem_params(16),
        cost_estimate=pl.CostEstimate(
            flops=2 * count * rows * FEAT * FEAT * 3 // 4,
            bytes_accessed=count * (rows * FEAT * 2 + FEAT * HALF * 2),
            transcendentals=0,
        ),
        name="gram",
    )(meta, pltpu.with_memory_space_constraint(stored, pltpu.HBM), *ties)


def side_kernel(count, *refs):
    out = refs[-1]
    for i in range(count):
        out[:, i] = refs[i][...]


def side_by_side(arrays, ties):
    whole = pl.BlockSpec(memory_space=pltpu.VMEM)
    first = arrays[0]
    return pl.pallas_call(
        functools.partial(side_kernel, len(arrays)),
        in_specs=[whole] * len(arrays) + [pl.BlockSpec(memory_space=pl.ANY)] * len(ties),
        out_shape=jax.ShapeDtypeStruct((first.shape[0], len(arrays)) + first.shape[1:], first.dtype),
        compiler_params=vmem_params(8),
        cost_estimate=small_cost(*arrays),
        name="side_by_side",
    )(*arrays, *ties)


def forward_kernel(y0, yb, x0, xb, tie, for_x, for_y):
    for_x[0] = y0[0]
    for_x[1:] = yb[0]
    for_y[0] = x0[0]
    for_y[1:] = xb[0]


def forward(x0, xb, y0, yb, tie):
    depth, width = x0.shape[1:]
    count = xb.shape[1]
    out = jax.ShapeDtypeStruct((count + 1, depth, width), x0.dtype)

    def spec(shape, first):
        return pl.BlockSpec((1,) + shape[1:], lambda i: (first,) + (0,) * (len(shape) - 1))

    return pl.pallas_call(
        forward_kernel,
        grid=(1,),
        in_specs=[spec(y0.shape, 0), spec(yb.shape, 0), spec(x0.shape, 1), spec(xb.shape, 1)]
        + [pl.BlockSpec(memory_space=pl.ANY)],
        out_specs=[pl.BlockSpec(out.shape, lambda i: (0, 0, 0))] * 2,
        out_shape=[out] * 2,
        compiler_params=vmem_params(16),
        cost_estimate=small_cost(x0, xb),
        name="forward",
    )(y0, yb, x0, xb, tie)


def pass_kernel(o1, o2, from_x, from_y, *refs):
    for_x, for_y = refs[-2:]
    half = BLOCK // 2
    f32 = jnp.float32
    for_x[:, :half] = o1[:, :half]
    for_x[:, half:] = (o1[:, half:].astype(f32) + from_y[...].astype(f32)).astype(jnp.bfloat16)
    for_y[:, :half] = (o2[:, :half].astype(f32) + from_x[...].astype(f32)).astype(jnp.bfloat16)
    for_y[:, half:] = o2[:, half:]


def pass_on(o1, o2, from_x, from_y, ties=()):
    return pl.pallas_call(
        pass_kernel,
        in_specs=[pl.BlockSpec(memory_space=pltpu.VMEM)] * 4
        + [pl.BlockSpec(memory_space=pl.ANY)] * len(ties),
        out_shape=[jax.ShapeDtypeStruct(o1.shape, o1.dtype)] * 2,
        compiler_params=vmem_params(8),
        cost_estimate=small_cost(o1, o2, o1, o2),
        name="pass_on",
    )(o1, o2, from_x, from_y, *ties)


def close_kernel(slots, count, o0, got_x, got_y, extra, *refs):
    arrived, outs = refs[:count], refs[-len(slots) :]
    f32 = jnp.float32
    for i, out in zip(slots, outs):
        total = o0[i].astype(f32) + got_x[i].astype(f32) + got_y[i].astype(f32)
        if not count:
            out[:BLOCK] = total.astype(jnp.bfloat16)
            out[BLOCK:] = extra[i]
            continue
        diag = diag_of_rows(extra[i])
        for other in arrived:
            total = total + other[:BLOCK].astype(f32)
            diag = diag + diag_of_rows(other[BLOCK:])
        out[:BLOCK] = total.astype(jnp.bfloat16)
        out[BLOCK:] = rows_of_diag(diag)


def close(o0, got_x, got_y, extra, slots, arrived=(), ties=()):
    return pl.pallas_call(
        functools.partial(close_kernel, slots, len(arrived)),
        in_specs=[pl.BlockSpec(memory_space=pltpu.VMEM)] * (4 + len(arrived))
        + [pl.BlockSpec(memory_space=pl.ANY)] * len(ties),
        out_shape=[jax.ShapeDtypeStruct((BLOCK + EXTRA, HALF), jnp.bfloat16)] * len(slots),
        compiler_params=vmem_params(8),
        cost_estimate=small_cost(o0, got_x, got_y, *arrived),
        name="close",
    )(o0, got_x, got_y, extra, *arrived, *ties)


def project_kernel(meta_ref, own0, own_b, x0, xb, y0, yb, opp_x, opp_y, *refs):
    rest, out = refs[:-1], refs[-1]
    parts = len(rest) // 2
    depth = own0.shape[1]
    for which in range(2):
        weights = []
        for r0, rb in ((own0, own_b), (x0, xb), (y0, yb)):
            weights.append([r0.at[which]] + [rb.at[which, i] for i in range(3)])
        opp = (opp_x, opp_y)[which]
        weights.append([opp.at[i] for i in range(4)])
        for part in range(parts):
            rows = rest[which * parts + part]
            total = None
            for corner in range(4):
                for i in range(4):
                    at = pl.multiple_of(meta_ref[corner * 4 + i] * depth, depth)
                    term = jnp.dot(
                        rows[:, pl.ds(at, depth)],
                        weights[corner][i][...],
                        preferred_element_type=jnp.float32,
                    )
                    total = term if total is None else total + term
            out[which, part] = total


def project(pieces, x_parts, g_parts, planes, corner):
    width = pieces[0].shape[-1]
    tok_count = x_parts[0].shape[0]
    meta = jnp.stack([4 * p + (corner ^ j) for j in range(4) for p in planes]).astype(jnp.int32)
    depth = pieces[0].shape[1]
    return pl.pallas_call(
        project_kernel,
        in_specs=[pl.BlockSpec(memory_space=pltpu.SMEM)]
        + [pl.BlockSpec(memory_space=pltpu.VMEM)] * (len(pieces) + 2 * len(x_parts)),
        out_shape=jax.ShapeDtypeStruct((2, len(x_parts), tok_count, width), jnp.float32),
        compiler_params=vmem_params(24),
        cost_estimate=pl.CostEstimate(
            flops=2 * 2 * len(x_parts) * tok_count * 16 * depth * width,
            bytes_accessed=2 * (2 * len(x_parts) * tok_count + 2 * width) * 16 * depth,
            transcendentals=0,
        ),
        name="project",
    )(meta, *pieces, *x_parts, *g_parts)


def gradient_kernel(meta_ref, total_ref, *refs):
    parts = total_ref.shape[1]
    marks, outs = refs[:parts], refs[parts:]
    width = total_ref.shape[3]
    xp = jnp.concatenate([total_ref[0, p].astype(jnp.bfloat16) for p in range(parts)], axis=0)
    gp = jnp.concatenate([total_ref[1, p].astype(jnp.bfloat16) for p in range(parts)], axis=0)
    tok_count = total_ref.shape[2]
    doc = lax.broadcasted_iota(jnp.int32, (EXTRA, tok_count), 0)
    weight = jnp.concatenate(
        [
            jnp.where((m[0:1, :] == doc) & (m[1:2, :] == 1), 1.0, 0.0).astype(jnp.bfloat16)
            for m in marks
        ],
        axis=1,
    )
    row = lax.broadcasted_iota(jnp.int32, (width, FEAT), 0)
    col = lax.broadcasted_iota(jnp.int32, (width, FEAT), 1)
    for r, out in enumerate(outs):
        at = row - RANK * meta_ref[r]
        pick_x = jnp.where(at == lax.rem(col, RANK), 1.0, 0.0).astype(jnp.bfloat16)
        pick_g = jnp.where(at == col // RANK, 1.0, 0.0).astype(jnp.bfloat16)
        x_wide = jnp.dot(xp, pick_x, preferred_element_type=jnp.float32)
        g_wide = jnp.dot(gp, pick_g, preferred_element_type=jnp.float32)
        product = x_wide * g_wide
        high = product.astype(jnp.bfloat16)
        low = (product - high.astype(jnp.float32)).astype(jnp.bfloat16)
        both = jnp.dot(weight, high, preferred_element_type=jnp.float32)
        both = both + jnp.dot(weight, low, preferred_element_type=jnp.float32)
        out[...] = both[:DOCS]


def gradients(total, marks, line, modules):
    meta = jnp.stack([lax.rem(line + r, modules) for r in range(modules)]).astype(jnp.int32)
    return pl.pallas_call(
        gradient_kernel,
        in_specs=[pl.BlockSpec(memory_space=pltpu.SMEM)]
        + [pl.BlockSpec(memory_space=pltpu.VMEM)] * (1 + len(marks)),
        out_shape=[jax.ShapeDtypeStruct((DOCS, FEAT), jnp.float32)] * modules,
        compiler_params=vmem_params(16),
        cost_estimate=pl.CostEstimate(
            flops=4 * modules * 256 * 128 * FEAT, bytes_accessed=4 * FEAT * 128, transcendentals=0
        ),
        name="gradients",
    )(meta, total, *marks)


def corner_richardson_kernel(total_rows, meta_ref, own, across, along, opp_a, opp_b, *refs):
    q_refs, (out_ref, pack_ref, full_ref) = refs[:-3], refs[-3:]
    pack_ref[meta_ref[0]] = own[:BLOCK]
    pack_ref[meta_ref[1]] = across[:BLOCK]
    pack_ref[meta_ref[2]] = along[:BLOCK]
    pack_ref[meta_ref[3], : BLOCK // 2] = opp_a[...]
    pack_ref[meta_ref[3], BLOCK // 2 :] = opp_b[: BLOCK // 2]
    packed = pack_ref[...].reshape(FEAT, HALF)
    at_row = lax.broadcasted_iota(jnp.int32, (HALF, HALF), 0)
    at_col = lax.broadcasted_iota(jnp.int32, (HALF, HALF), 1)
    both = packed[HALF:].astype(jnp.float32)
    both_t = both.T
    zero = jnp.zeros_like(both)
    above, below = at_row < at_col, at_row > at_col
    full_ref[:HALF, :HALF] = jnp.where(above, both, jnp.where(below, both_t, zero)).astype(jnp.bfloat16)
    full_ref[HALF:, HALF:] = jnp.where(below, both, jnp.where(above, both_t, zero)).astype(jnp.bfloat16)
    cross = packed[:HALF]
    full_ref[:HALF, HALF:] = cross
    full_ref[HALF:, :HALF] = cross.astype(jnp.float32).T.astype(jnp.bfloat16)
    diag = diag_of_rows(own[BLOCK:]) + diag_of_rows(across[BLOCK:])
    diag = diag + (diag_of_rows(along[BLOCK:]) + diag_of_rows(opp_b[BLOCK // 2 :]))
    diag = jnp.concatenate([diag[0:1], diag[1:2]], axis=1) / total_rows
    mean_diag = jnp.sum(diag, axis=1, keepdims=True) / FEAT
    step_size = 1.0 / (spread * (mean_diag + epsilon))
    own_diag = diag + damping * mean_diag
    lines = len(q_refs)
    queries = jnp.concatenate([q[...] for q in q_refs], axis=0)
    count = queries.shape[0]
    v = step_size * queries
    for _ in range(STEPS):
        high = v.astype(jnp.bfloat16)
        rest = v - high.astype(jnp.float32)
        mid = rest.astype(jnp.bfloat16)
        low = (rest - mid.astype(jnp.float32)).astype(jnp.bfloat16)
        parts = jnp.concatenate([high, mid, low], axis=0)
        off = jnp.dot(parts, full_ref[...], preferred_element_type=jnp.float32)
        off = off[:count] + (off[count : 2 * count] + off[2 * count :])
        v = v + step_size * (queries - (off / total_rows + own_diag * v))
    to = lax.broadcasted_iota(jnp.int32, (count, count), 0)
    at = lax.broadcasted_iota(jnp.int32, (count, count), 1)
    source = jnp.zeros((count, count), jnp.int32)
    for r in range(lines):
        here = (to >= DOCS * meta_ref[4 + r]) & (to < DOCS * (meta_ref[4 + r] + 1))
        source = jnp.where(here, to + DOCS * (r - meta_ref[4 + r]), source)
    order = jnp.where(at == source, 1.0, 0.0).astype(jnp.bfloat16)
    out_ref[...] = jnp.dot(order, v.astype(jnp.bfloat16), preferred_element_type=jnp.float32).astype(
        jnp.bfloat16
    )


def corner_precondition(total_rows, pieces, corner, line, queries):
    lines = len(queries)
    meta = jnp.stack(
        [corner ^ j for j in range(4)] + [lax.rem(line - r + lines, lines) for r in range(lines)]
    ).astype(jnp.int32)
    count = lines * DOCS
    return pl.pallas_call(
        functools.partial(corner_richardson_kernel, total_rows),
        in_specs=[pl.BlockSpec(memory_space=pltpu.SMEM)]
        + [pl.BlockSpec(memory_space=pltpu.VMEM)] * (5 + lines),
        out_shape=jax.ShapeDtypeStruct((count, FEAT), jnp.bfloat16),
        scratch_shapes=[
            pltpu.VMEM((4, BLOCK, HALF), jnp.bfloat16),
            pltpu.VMEM((FEAT, FEAT), jnp.bfloat16),
        ],
        compiler_params=vmem_params(16),
        cost_estimate=pl.CostEstimate(
            flops=2 * STEPS * 3 * count * FEAT * FEAT, bytes_accessed=4 * FEAT * FEAT, transcendentals=0
        ),
        name="richardson",
    )(meta, *pieces, *queries)


def corner_score_kernel(scale, meta_ref, *refs):
    pieces, streams, (mine_ref, other_ref, flat_ref) = refs[:4], refs[4:-3], refs[-3:]
    lines, count, _ = pieces[0].shape

    @pl.when(pl.program_id(0) == 0)
    def _():
        for j, piece in enumerate(pieces):
            at = pl.multiple_of(meta_ref[j] * count, count)
            for s in range(lines):
                flat_ref[meta_ref[4 + s], pl.ds(at, count)] = piece[s]

    scores = None
    for m, s_ref in enumerate(streams):
        term = lax.dot_general(
            s_ref[...], flat_ref[m], (((1,), (1,)), ((), ())), preferred_element_type=jnp.float32
        )
        scores = term if scores is None else scores + term
    scores = scale * scores.T
    rows = [
        scores[k * count + z * DOCS : k * count + (z + 1) * DOCS] for z in range(lines) for k in range(4)
    ]
    half = len(rows) // 2
    low, high = jnp.concatenate(rows[:half], axis=0), jnp.concatenate(rows[half:], axis=0)
    first = meta_ref[4 + lines] == 0
    mine_ref[...] = jnp.where(first, low, high)
    other_ref[...] = jnp.where(first, high, low)


def corner_score(pieces, stored, corner, line, scale):
    lines, count, _ = pieces[0].shape
    rows, width = stored.shape
    total = 4 * count
    tile = 512
    modules = width // FEAT
    meta = jnp.stack(
        [corner ^ j for j in range(4)]
        + [lax.rem(line - s + lines, lines) for s in range(lines)]
        + [lax.axis_index("ctx")]
    ).astype(jnp.int32)
    shape = (total // 2, rows)

    def module_columns(m):
        return pl.BlockSpec((tile, FEAT), lambda i, meta: (i, m))

    stored = pltpu.with_memory_space_constraint(stored, pltpu.HBM)
    return pl.pallas_call(
        functools.partial(corner_score_kernel, scale),
        grid_spec=pltpu.PrefetchScalarGridSpec(
            num_scalar_prefetch=1,
            grid=(rows // tile,),
            in_specs=[pl.BlockSpec(p.shape, lambda i, meta: (0, 0, 0)) for p in pieces]
            + [module_columns(m) for m in range(modules)],
            out_specs=[pl.BlockSpec((shape[0], tile), lambda i, meta: (0, i))] * 2,
            scratch_shapes=[pltpu.VMEM((modules, total, FEAT), jnp.bfloat16)],
        ),
        out_shape=[jax.ShapeDtypeStruct(shape, jnp.float32)] * 2,
        compiler_params=vmem_params(24),
        cost_estimate=pl.CostEstimate(
            flops=2 * total * width * rows, bytes_accessed=2 * rows * width, transcendentals=0
        ),
        name="score",
    )(meta, *pieces, *[stored] * modules)


def to_corner(value, n_ex, bit):
    return lax.ppermute(value, "ex", [(e, e ^ bit) for e in range(n_ex)])


def to_plane(value, n_ex, shift):
    return lax.ppermute(value, "ex", [(e, (e + 4 * shift) % n_ex) for e in range(n_ex)])


def shards(acts, out_grads, projections, segments, valid, stored):
    n_ex = lax.axis_size("ex")
    n_ctx = lax.axis_size("ctx")
    mod_dev = projections.shape[2] // RANK
    if mod_dev != 4 or n_ex != 16 or n_ctx != 2:
        return general(acts, out_grads, projections, segments, valid, stored)
    lines = n_ex // 4
    tok_count = acts.shape[1]
    me = lax.axis_index("ex")
    line, corner = me // 4, lax.rem(me, 4)

    def gram(planes, ties):
        return block_gram(stored, [lax.rem(line + r, lines) for r in planes], corner, ties)

    line1, line3, line2 = (to_plane(projections, n_ex, s) for s in (1, 3, 2))
    x0, y0 = to_corner(projections, n_ex, 1), to_corner(projections, n_ex, 2)
    o0, o1, o2, o3a, o3b, extra = gram((1, 2), [])
    own_b = side_by_side([line1, line3, line2], [extra, x0, y0])
    x_rows, g_rows, _ = lax.optimization_barrier((acts[0], out_grads[0], own_b))
    x_parts, g_parts = swapped(x_rows, n_ctx), swapped(g_rows, n_ctx)
    from_x, from_y = to_corner(o3a, n_ex, 1), to_corner(o3b, n_ex, 2)
    xb, yb = to_corner(own_b, n_ex, 1), to_corner(own_b, n_ex, 2)
    p0, p1, p2, p3a, p3b, extra_b = gram((3, 0), [own_b, x0, y0])
    marks = swapped(jnp.concatenate([segments, valid], axis=0), n_ctx)
    for_x, for_y = pass_on(o1, o2, from_x, from_y, (extra_b, x_parts[1], g_parts[1]))
    got_x, got_y = to_corner(for_x, n_ex, 1), to_corner(for_y, n_ex, 2)
    from_xb, from_yb = to_corner(p3a, n_ex, 1), to_corner(p3b, n_ex, 2)
    opp_x, opp_y = forward(x0, xb, y0, yb, for_x)
    opp_x, opp_y = to_corner(opp_x, n_ex, 1), to_corner(opp_y, n_ex, 2)

    planes = [lax.rem(line - s + lines, lines) for s in (0, 1, 3, 2)]
    total = project((projections, own_b, x0, xb, y0, yb, opp_x, opp_y), x_parts, g_parts, planes, corner)
    docs = gradients(total, marks, line, mod_dev)
    queries = [docs[0]] + [to_plane(docs[s], n_ex, s) for s in range(1, lines)]

    message1, message2 = close(o0, got_x, got_y, extra, (0, 1))
    for_xb, for_yb = pass_on(p1, p2, from_xb, from_yb, (got_x, got_y))
    got_xb, got_yb = to_corner(for_xb, n_ex, 1), to_corner(for_yb, n_ex, 2)
    sent = [to_plane(message1, n_ex, 1), to_plane(message2, n_ex, 2)]
    (message3,) = close(p0, got_xb, got_yb, extra_b, (0,))
    sent.append(to_plane(message3, n_ex, 3))
    (kept,) = close(p0, got_xb, got_yb, extra_b, (1,), sent, (docs[0],))

    kept_x, kept_y = to_corner(kept, n_ex, 1), to_corner(kept, n_ex, 2)
    opp_a = to_corner(kept_y[: BLOCK // 2], n_ex, 1)
    opp_b = to_corner(kept_x[BLOCK // 2 :], n_ex, 2)

    total_rows = stored.shape[0] * n_ex
    precond = corner_precondition(
        float(total_rows), (kept, kept_x, kept_y, opp_a, opp_b), corner, line, queries
    )

    stack = jnp.stack([precond] + [to_plane(precond, n_ex, s) for s in range(1, lines)])
    pieces = [stack] + [to_corner(stack, n_ex, bit) for bit in (1, 2, 3)]
    scale = 1.0 / math.sqrt(MODULES * FEAT * tok_count * n_ctx / DOCS)
    mine, other = corner_score(pieces, stored, corner, line, scale)
    return mine + lax.ppermute(other, "ctx", [(0, 1), (1, 0)])


def solution(mesh):
    in_specs = (
        P("ex", "ctx", None),
        P("ex", "ctx", None),
        P(None, "ex", "ctx"),
        P("ex", "ctx"),
        P("ex", "ctx"),
        P("ex", "ctx"),
    )
    out_specs = P("ctx", "ex")
    return jax.shard_map(shards, mesh=mesh, in_specs=in_specs, out_specs=out_specs, check_vma=False)
```
